32 devices in a mesh: groups: 2 (over y), cls: 4 (over z), rep: 4 (over x, core).
Axes of the slice: x: 2, y: 2, z: 4, core: 2. Of those that a mesh axis runs over, the one named last changes fastest.
Arguments:
- particles: bfloat16 [1024, 256, 256], P(('groups', 'cls', 'rep')), parts along dimension 0, may hold values from -6 to 6
- classes: int32 [1024], P(('groups', 'cls', 'rep')), parts along dimension 0, may hold values from 0 to 23, as said below
- rotation: int32 [1024], P(('groups', 'cls', 'rep')), parts along dimension 0, may hold values from 0 to 7
- defocus: int32 [1024], P(('groups', 'cls', 'rep')), parts along dimension 0, may hold values from 0 to 3
- filter_taps: float32 [31], replicated, may hold values from -1 to 1
- ctf_table: bfloat16 [4, 256, 256], replicated, may hold values from -1.01 to 1.01
- references: bfloat16 [48, 256, 256], P(('groups', 'cls'), 'rep'), parts along dimension 0, may hold values from -6 to 6
Outputs:
- new_references: float32 [48, 256, 256], P(('groups', 'cls'), 'rep'), parts along dimension 0
The draws below stay inside these ranges and needn't reach their ends.
There are 2 independent parts, one for each index of `groups`. The reference program is written for one: setup_inputs(seed, part) draws one part's arguments, and reference() takes and returns one part's arrays. A program takes and returns all parts, laid end to end along the dimension named above; an argument that names none is the same for every part. Nothing has to cross between parts.
Inputs may be any that keep to these rules, and one draw needn't show every extreme that they name: Among the 32 particles of one device (aligned blocks of 32 rows in order), at most 16 are assigned to classes of one index o of cls, the classes o * 6 to o * 6 + 5; in every such block some index receives exactly 16.
All inputs are finite; a program needn't handle non-finite values.
Results may differ from the reference program's by a relative error of at most 0.0065.
Values may be sent and summed in bfloat16 or wider, within the bound.
A program may use at most 64 MiB of HBM per device.

```python
import math
import jax
import jax.numpy as jnp
from jax import lax

TILE = 256
TAPS = 31
BINS = 4
CLS_DEV = 6
P_DEV = 32
CLASSES = 24
CAP = 16
PARTICLES = 512
N_CLS = 4
N_REP = 4


def draw_classes(key, part):
    blocks = N_CLS * N_REP
    slot_count = N_CLS * CAP
    hot_key, block_key = jax.random.split(key)
    penalty = jax.random.randint(hot_key, (N_CLS,), 0, 3) * 1024
    slot_owner = jnp.arange(slot_count, dtype=jnp.int32) // CAP

    def one_block(sub_key, block_id):
        pick_key, score_key, local_key, order_key = jax.random.split(sub_key, 4)
        forced = jax.random.randint(pick_key, (), 0, N_CLS)
        forced = jnp.where(block_id == 0, N_CLS - 1, jnp.where(block_id == 1, 0, forced))
        priority = jax.random.randint(score_key, (slot_count,), 0, 1024) + penalty[slot_owner]
        priority = jnp.where(slot_owner == forced, -1, priority)
        ranking = jnp.argsort(priority * slot_count + jnp.arange(slot_count, dtype=jnp.int32))
        picked = slot_owner[ranking[:P_DEV]]
        local_ids = jax.random.randint(local_key, (P_DEV,), 0, CLS_DEV)
        first_local = jnp.where(block_id == 0, CLS_DEV - 1, jnp.where(block_id == 1, 0, local_ids[0]))
        local_ids = local_ids.at[0].set(first_local)
        labels = picked * CLS_DEV + local_ids
        return labels[jax.random.permutation(order_key, P_DEV)]
    block_keys = jax.random.split(block_key, blocks)
    return jax.vmap(one_block)(block_keys, jnp.arange(blocks, dtype=jnp.int32)).reshape(-1)


def draw_ctf_table(key, part):
    defocus_key, decay_key = jax.random.split(key)
    pixel_index = jnp.arange(TILE, dtype=jnp.int32)
    frequency = jnp.minimum(pixel_index, TILE - pixel_index).astype(jnp.float32) / TILE
    radius_sq = frequency[:, None] * frequency[:, None] + frequency[None, :] * frequency[None, :]
    defocus_scale = jax.random.uniform(defocus_key, (BINS,), minval=100.0, maxval=600.0)
    decay = jax.random.uniform(decay_key, (BINS,), minval=1.0, maxval=4.0)
    phase = math.pi * defocus_scale[:, None, None] * radius_sq[None]
    envelope = jnp.exp(-decay[:, None, None] * radius_sq[None])
    return (-(0.995 * jnp.sin(phase) + 0.1 * jnp.cos(phase)) * envelope).astype(jnp.bfloat16)


def set_ends(array, key, smallest, top_value):
    dims = array.shape
    place = [jax.random.randint(jax.random.fold_in(key, axis), (), 0, dims[axis]) for axis in range(len(dims))]
    array = array.at[tuple(place)].set(smallest)
    longest = dims.index(max(dims))
    place[longest] = (place[longest] + 1) % dims[longest]
    return array.at[tuple(place)].set(top_value)


def level_of(key, dims, pieces, least, high):
    gain = 1.0
    for position, shards_of in pieces:
        heights = jax.random.uniform(jax.random.fold_in(jax.random.fold_in(key, 6), position), (shards_of,), jnp.float32, least / len(pieces), high / len(pieces))
        gain = gain * jnp.repeat(jnp.exp(heights), dims[position] // shards_of).reshape((-1,) + (1,) * (len(dims) - 1 - position))
    return gain


def noise(key, dims, deviation, bound, cuts=(), kind=jnp.bfloat16):
    entries = jax.random.normal(key, dims, jnp.float32) * deviation
    if len(cuts) > 0:
        entries = level_of(key, dims, cuts, -0.22, 0.18) * entries
    return jnp.clip(entries, min=-bound, max=bound).astype(kind)


def setup_inputs(seed: int = 0, part: int = 0) -> dict:
    splits = jax.random.split(jax.random.key(seed), 8)
    part_splits = jax.random.split(jax.random.fold_in(splits[7], part), 8)
    particles = noise(part_splits[0], (PARTICLES, TILE, TILE), 1.0, 6.0, ((0, 16),))
    classes = draw_classes(jax.random.fold_in(jax.random.fold_in(splits[7], part), 71), part)
    rotation = set_ends(jax.random.randint(part_splits[2], (PARTICLES,), 0, 8), jax.random.fold_in(part_splits[2], 1), 0, 7).astype(jnp.int32)
    defocus = set_ends(jax.random.randint(part_splits[3], (PARTICLES,), 0, BINS), jax.random.fold_in(part_splits[3], 1), 0, BINS - 1).astype(jnp.int32)
    filter_taps = noise(splits[4], (TAPS,), TAPS ** -0.5, 1.0, (), jnp.float32)
    ctf_table = draw_ctf_table(jax.random.fold_in(splits[7], 71), part)
    references = noise(part_splits[6], (CLASSES, TILE, TILE), 1.0, 6.0, ((0, 4), (1, 4)))
    return dict(particles=particles, classes=classes, rotation=rotation, defocus=defocus, filter_taps=filter_taps, ctf_table=ctf_table, references=references)


EPSILON = 1e-05
PRIOR_WEIGHT = 4.0

def hartley_table(tile_len):
    pixel_index = jnp.arange(tile_len, dtype=jnp.int32)
    product = pixel_index[:, None] * pixel_index[None, :] % tile_len
    phases = 2.0 * math.pi / tile_len * product.astype(jnp.float32)
    return jnp.cos(phases) + jnp.sin(phases)

def band_table(filter_taps, tile_len):
    half_width = (filter_taps.shape[0] - 1) // 2
    matrix = jnp.zeros((tile_len, tile_len), jnp.float32)
    for offset in range(filter_taps.shape[0]):
        matrix = matrix + filter_taps[offset] * jnp.eye(tile_len, k=offset - half_width, dtype=jnp.float32)
    return matrix

def orient(tile_block, turn_codes):
    transpose_mask = (turn_codes >= 4)[:, None, None]
    flip_rows = (turn_codes % 2 == 1)[:, None, None]
    flip_cols = (turn_codes // 2 % 2 == 1)[:, None, None]
    turned = jnp.where(transpose_mask, jnp.swapaxes(tile_block, 1, 2), tile_block)
    turned = jnp.where(flip_rows, turned[:, ::-1, :], turned)
    return jnp.where(flip_cols, turned[:, :, ::-1], turned)

def prepare(tile_block, turn_codes, spectral_gain, analysis, synthesis):
    tile_len = tile_block.shape[1]
    oriented = orient(tile_block, turn_codes).astype(jnp.float32)
    analysis_f = analysis.astype(jnp.float32)
    synthesis_f = synthesis.astype(jnp.float32)
    first_pass = jnp.einsum('pij,lj->pil', oriented, analysis_f).astype(jnp.bfloat16)
    raw_spectra = jnp.einsum('li,pim->plm', analysis_f, first_pass.astype(jnp.float32))
    spectra = (raw_spectra * spectral_gain).astype(jnp.bfloat16)
    second_pass = jnp.einsum('pkm,my->pky', spectra.astype(jnp.float32), synthesis_f).astype(jnp.bfloat16)
    result = jnp.einsum('xk,pky->pxy', synthesis_f, second_pass.astype(jnp.float32)) / (tile_len * tile_len)
    return result.astype(jnp.bfloat16)

def reference(particles, classes, rotation, defocus, filter_taps, ctf_table, references):
    hartley = hartley_table(TILE)
    analysis = jnp.dot(hartley, band_table(filter_taps, TILE), preferred_element_type=jnp.float32, precision=lax.Precision.HIGHEST).astype(jnp.bfloat16)
    synthesis = hartley.astype(jnp.bfloat16)
    ref_f = references.astype(jnp.float32)
    ref_power = lax.optimization_barrier(jnp.mean(ref_f * ref_f, axis=(1, 2)))
    blocks = PARTICLES // P_DEV

    def accumulate_block(running, inputs):
        tile_block, class_ids, turn_codes, bin_ids = inputs
        spectral_gain = ctf_table[bin_ids].astype(jnp.float32)
        filtered = prepare(tile_block, turn_codes, spectral_gain, analysis, synthesis)
        filt_f = filtered.astype(jnp.float32)
        tile_power = lax.optimization_barrier(jnp.mean(filt_f * filt_f, axis=(1, 2)))
        chosen = references[class_ids].astype(jnp.float32)
        intersection = lax.optimization_barrier(jnp.mean(filt_f * chosen, axis=(1, 2)))
        scores = intersection / jnp.sqrt((tile_power + EPSILON) * (ref_power[class_ids] + EPSILON))
        weight = jax.nn.sigmoid(TILE * scores)
        scaling = (weight / jnp.sqrt(tile_power + EPSILON)).astype(jnp.bfloat16)
        scaling = lax.optimization_barrier(scaling).astype(jnp.float32)
        class_sums, class_weights = running
        class_sums = class_sums.at[class_ids].add(scaling[:, None, None] * filt_f)
        class_weights = class_weights.at[class_ids].add(weight)
        return ((class_sums, class_weights), None)
    starting = (jnp.zeros((CLASSES, TILE, TILE), jnp.float32), jnp.zeros((CLASSES,), jnp.float32))
    inputs = (particles.reshape(blocks, P_DEV, TILE, TILE), classes.reshape(blocks, P_DEV), rotation.reshape(blocks, P_DEV), defocus.reshape(blocks, P_DEV))
    (class_sums, class_weights), _ = lax.scan(accumulate_block, starting, inputs)
    return (PRIOR_WEIGHT * ref_f + class_sums) / (PRIOR_WEIGHT + class_weights[:, None, None])
```

```python
import functools
import math

import numpy as np

import jax
import jax.numpy as jnp
from jax import lax
from jax.experimental import pallas as pl
from jax.experimental.pallas import tpu as pltpu
from jax.sharding import PartitionSpec as P

EPSILON = 1e-05
PRIOR_WEIGHT = 4.0
F32 = jnp.float32
BF16 = jnp.bfloat16
MIB = 1 << 20


def hartley_table(tile_len):
    index = np.arange(tile_len, dtype=np.int64)
    phases = 2.0 * np.pi / tile_len * (index[:, None] * index[None, :] % tile_len)
    return (np.cos(phases) + np.sin(phases)).astype(np.float32)


def filter_kernel(
    turn_ref, bin_ref, taps_ref, hartley_ref, ctf_ref, tile_ref, out_ref, fwd, fwd_t, syn
):
    batch, tile_len, _ = tile_ref.shape
    taps = taps_ref.shape[0]
    half = (taps - 1) // 2
    step = pl.program_id(0)

    @pl.when(step == 0)
    def _():
        row = lax.broadcasted_iota(jnp.int32, (tile_len, tile_len), 0)
        col = lax.broadcasted_iota(jnp.int32, (tile_len, tile_len), 1)
        gap = col - row
        band = jnp.zeros((tile_len, tile_len), F32)
        for tap in range(taps):
            band = jnp.where(gap == tap - half, taps_ref[tap], band)
        hartley = hartley_ref[...]
        analysis = jnp.dot(
            hartley, band, preferred_element_type=F32, precision=lax.Precision.HIGHEST
        ).astype(BF16)
        mirror = jnp.where(row + col == tile_len - 1, 1.0, 0.0).astype(BF16)
        mirrored = jnp.dot(analysis, mirror, preferred_element_type=F32)
        fwd[0] = analysis
        fwd[1] = mirrored.astype(BF16)
        fwd_t[0] = analysis.astype(F32).T.astype(BF16)
        fwd_t[1] = mirrored.T.astype(BF16)
        syn[...] = hartley.astype(BF16)

    for i in range(batch):
        code = turn_ref[step * batch + i]
        tile = tile_ref[i]
        tile = jnp.where(code >= 4, tile.T, tile)
        first = jnp.dot(tile, fwd_t[(code // 2) % 2], preferred_element_type=F32).astype(BF16)
        raw = jnp.dot(fwd[code % 2], first, preferred_element_type=F32)
        gain = ctf_ref[bin_ref[step * batch + i]].astype(F32)
        spectra = (raw * gain).astype(BF16)
        second = jnp.dot(spectra, syn[...], preferred_element_type=F32).astype(BF16)
        result = jnp.dot(syn[...], second, preferred_element_type=F32)
        out_ref[i] = (result * (1.0 / (tile_len * tile_len))).astype(BF16)


def filter_tiles(particles, rotation, defocus, filter_taps, ctf_table):
    count, tile_len, _ = particles.shape
    batch = math.gcd(count, 4)
    hartley = jnp.asarray(hartley_table(tile_len))
    square = (tile_len, tile_len)
    grid_spec = pltpu.PrefetchScalarGridSpec(
        num_scalar_prefetch=3,
        grid=(count // batch,),
        in_specs=[
            pl.BlockSpec(square, lambda i, *_: (0, 0)),
            pl.BlockSpec(ctf_table.shape, lambda i, *_: (0, 0, 0)),
            pl.BlockSpec((batch,) + square, lambda i, *_: (i, 0, 0)),
        ],
        out_specs=pl.BlockSpec((batch,) + square, lambda i, *_: (i, 0, 0)),
        scratch_shapes=[
            pltpu.VMEM((2,) + square, BF16),
            pltpu.VMEM((2,) + square, BF16),
            pltpu.VMEM(square, BF16),
        ],
    )
    return pl.pallas_call(
        filter_kernel,
        grid_spec=grid_spec,
        out_shape=jax.ShapeDtypeStruct(particles.shape, BF16),
        compiler_params=pltpu.CompilerParams(vmem_limit_bytes=24 * MIB),
        cost_estimate=pl.CostEstimate(
            flops=8 * count * tile_len**3,
            bytes_accessed=4 * count * tile_len**2,
            transcendentals=0,
        ),
        name="filter_tiles",
    )(rotation, defocus, filter_taps, hartley, ctf_table, particles)


def weigh_kernel(class_ref, tile_ref, refs_ref, sum_ref, weight_ref, acc, start, order):
    count, tile_len, _ = tile_ref.shape
    _, reps, own, rows, _ = refs_ref.shape
    owners = pl.num_programs(0)
    owner = pl.program_id(0)
    scale = 1.0 / (tile_len * tile_len)

    @pl.when(owner == 0)
    def _():
        def clear(i, carry):
            start[i] = 0
            return carry

        lax.fori_loop(0, owners + 1, clear, 0)

        def tally(i, carry):
            slot = class_ref[i] // own + 1
            start[slot] = start[slot] + 1
            return carry

        lax.fori_loop(0, count, tally, 0)

        def running(i, carry):
            total = carry + start[i]
            start[i] = total
            return total

        lax.fori_loop(0, owners + 1, running, 0)

        def place(i, carry):
            slot = class_ref[i] // own
            where = start[slot]
            order[where] = i
            start[slot] = where + 1
            return carry

        lax.fori_loop(0, count, place, 0)

    end = start[owner]
    begin = jnp.where(owner == 0, 0, start[jnp.maximum(owner - 1, 0)])
    acc[...] = jnp.zeros_like(acc)
    weight_ref[...] = jnp.zeros_like(weight_ref)
    row = lax.broadcasted_iota(jnp.int32, weight_ref.shape[1:], 0)

    def total(values):
        return jnp.sum(jnp.sum(values, axis=0, keepdims=True), axis=1, keepdims=True)

    def body(i, carry):
        p = order[i]
        k = class_ref[p] - owner * own
        tile = tile_ref[p].astype(F32)
        image = refs_ref[0, :, k].reshape(tile_len, tile_len).astype(F32)
        power = total(tile * tile) * scale
        ref_power = total(image * image) * scale
        meet = total(tile * image) * scale
        score = meet / jnp.sqrt((power + EPSILON) * (ref_power + EPSILON))
        weight = 1.0 / (1.0 + jnp.exp(-tile_len * score))
        scaling = (weight / jnp.sqrt(power + EPSILON)).astype(BF16).astype(F32)
        acc[k] += scaling * tile
        weight_ref[0] += jnp.where(row == k, weight, 0.0)
        return carry

    lax.fori_loop(begin, end, body, 0)
    for k in range(own):
        sum_ref[0, :, k] = acc[k].astype(BF16).reshape(reps, rows, tile_len)


def weigh(filtered, classes, refs):
    count, tile_len, _ = filtered.shape
    owners, reps, own, rows, _ = refs.shape
    slots = -(-own // 8) * 8
    block = (1, reps, own, rows, tile_len)
    grid_spec = pltpu.PrefetchScalarGridSpec(
        num_scalar_prefetch=1,
        grid=(owners,),
        in_specs=[
            pl.BlockSpec(filtered.shape, lambda o, *_: (0, 0, 0)),
            pl.BlockSpec(block, lambda o, *_: (o, 0, 0, 0, 0)),
        ],
        out_specs=[
            pl.BlockSpec(block, lambda o, *_: (o, 0, 0, 0, 0)),
            pl.BlockSpec((1, slots, 128), lambda o, *_: (o, 0, 0)),
        ],
        scratch_shapes=[
            pltpu.VMEM((own, tile_len, tile_len), F32),
            pltpu.SMEM((owners + 1,), jnp.int32),
            pltpu.SMEM((count,), jnp.int32),
        ],
    )
    return pl.pallas_call(
        weigh_kernel,
        grid_spec=grid_spec,
        out_shape=[
            jax.ShapeDtypeStruct(refs.shape, BF16),
            jax.ShapeDtypeStruct((owners, slots, 128), F32),
        ],
        compiler_params=pltpu.CompilerParams(vmem_limit_bytes=32 * MIB),
        name="weigh_tiles",
    )(classes, filtered, refs)


def local(particles, classes, rotation, defocus, filter_taps, ctf_table, references):
    owners = lax.axis_size("cls")
    reps = lax.axis_size("rep")
    own, rows, tile_len = references.shape
    refs = lax.all_gather(references, ("cls", "rep"), axis=0, tiled=False)
    refs = refs.reshape(owners, reps, own, rows, tile_len)
    filtered = filter_tiles(particles, rotation, defocus, filter_taps, ctf_table)
    sums, weights = weigh(filtered, classes, refs)
    sums = lax.psum_scatter(sums, "rep", scatter_dimension=1, tiled=False)
    sums = lax.psum_scatter(sums, "cls", scatter_dimension=0, tiled=False)
    weights = lax.psum(weights[:, :own, 0], ("cls", "rep"))
    total = lax.dynamic_index_in_dim(weights, lax.axis_index("cls"), 0, keepdims=False)
    return (PRIOR_WEIGHT * references.astype(F32) + sums.astype(F32)) / (
        PRIOR_WEIGHT + total[:, None, None]
    )


def solution(mesh):
    placed = (
        P(("groups", "cls", "rep"), None, None),
        P(("groups", "cls", "rep")),
        P(("groups", "cls", "rep")),
        P(("groups", "cls", "rep")),
        P(),
        P(),
        P(("groups", "cls"), "rep", None),
    )
    return jax.shard_map(
        local,
        mesh=mesh,
        in_specs=placed,
        out_specs=P(("groups", "cls"), "rep", None),
        check_vma=False,
    )
```

```python
import functools
import math

import numpy as np

import jax
import jax.numpy as jnp
from jax import lax
from jax.experimental import pallas as pl
from jax.experimental.pallas import tpu as pltpu
from jax.sharding import PartitionSpec as P

EPSILON = 1e-05
PRIOR_WEIGHT = 4.0
F32 = jnp.float32
BF16 = jnp.bfloat16
MIB = 1 << 20


def hartley_table(tile_len):
    index = np.arange(tile_len, dtype=np.int64)
    phases = 2.0 * np.pi / tile_len * (index[:, None] * index[None, :] % tile_len)
    return (np.cos(phases) + np.sin(phases)).astype(np.float32)


def filter_kernel(
    turn_ref, bin_ref, taps_ref, hartley_ref, ctf_ref, tile_ref, out_ref, fwd, fwd_t, syn
):
    batch, tile_len, _ = tile_ref.shape
    taps = taps_ref.shape[0]
    half = (taps - 1) // 2
    step = pl.program_id(0)

    @pl.when(step == 0)
    def _():
        row = lax.broadcasted_iota(jnp.int32, (tile_len, tile_len), 0)
        col = lax.broadcasted_iota(jnp.int32, (tile_len, tile_len), 1)
        gap = col - row
        band = jnp.zeros((tile_len, tile_len), F32)
        for tap in range(taps):
            band = jnp.where(gap == tap - half, taps_ref[tap], band)
        hartley = hartley_ref[...]
        analysis = jnp.dot(
            hartley, band, preferred_element_type=F32, precision=lax.Precision.HIGHEST
        ).astype(BF16)
        mirror = jnp.where(row + col == tile_len - 1, 1.0, 0.0).astype(BF16)
        mirrored = jnp.dot(analysis, mirror, preferred_element_type=F32)
        fwd[0] = analysis
        fwd[1] = mirrored.astype(BF16)
        fwd_t[0] = analysis.astype(F32).T.astype(BF16)
        fwd_t[1] = mirrored.T.astype(BF16)
        syn[...] = hartley.astype(BF16)

    for i in range(batch):
        code = turn_ref[step * batch + i]
        tile = tile_ref[i]
        tile = jnp.where(code >= 4, tile.T, tile)
        first = jnp.dot(tile, fwd_t[(code // 2) % 2], preferred_element_type=F32).astype(BF16)
        raw = jnp.dot(fwd[code % 2], first, preferred_element_type=F32)
        gain = ctf_ref[bin_ref[step * batch + i]].astype(F32)
        spectra = (raw * gain).astype(BF16)
        second = jnp.dot(spectra, syn[...], preferred_element_type=F32).astype(BF16)
        result = jnp.dot(syn[...], second, preferred_element_type=F32)
        out_ref[i] = (result * (1.0 / (tile_len * tile_len))).astype(BF16)


def filter_tiles(particles, rotation, defocus, filter_taps, ctf_table):
    count, tile_len, _ = particles.shape
    batch = math.gcd(count, 4)
    hartley = jnp.asarray(hartley_table(tile_len))
    square = (tile_len, tile_len)
    grid_spec = pltpu.PrefetchScalarGridSpec(
        num_scalar_prefetch=3,
        grid=(count // batch,),
        in_specs=[
            pl.BlockSpec(square, lambda i, *_: (0, 0)),
            pl.BlockSpec(ctf_table.shape, lambda i, *_: (0, 0, 0)),
            pl.BlockSpec((batch,) + square, lambda i, *_: (i, 0, 0)),
        ],
        out_specs=pl.BlockSpec((batch,) + square, lambda i, *_: (i, 0, 0)),
        scratch_shapes=[
            pltpu.VMEM((2,) + square, BF16),
            pltpu.VMEM((2,) + square, BF16),
            pltpu.VMEM(square, BF16),
        ],
    )
    return pl.pallas_call(
        filter_kernel,
        grid_spec=grid_spec,
        out_shape=jax.ShapeDtypeStruct(particles.shape, BF16),
        compiler_params=pltpu.CompilerParams(vmem_limit_bytes=24 * MIB),
        cost_estimate=pl.CostEstimate(
            flops=8 * count * tile_len**3,
            bytes_accessed=4 * count * tile_len**2,
            transcendentals=0,
        ),
        name="filter_tiles",
    )(rotation, defocus, filter_taps, hartley, ctf_table, particles)


def weigh_kernel(class_ref, tile_ref, refs_ref, sum_ref, weight_ref, acc, start, order):
    count, tile_len, _ = tile_ref.shape
    _, reps, own, rows, _ = refs_ref.shape
    lanes = sum_ref.shape[1]
    owners = pl.num_programs(0)
    owner = pl.program_id(0)
    scale = 1.0 / (tile_len * tile_len)

    @pl.when(owner == 0)
    def _():
        def clear(i, carry):
            start[i] = 0
            return carry

        lax.fori_loop(0, owners + 1, clear, 0)

        def tally(i, carry):
            slot = class_ref[i] // own + 1
            start[slot] = start[slot] + 1
            return carry

        lax.fori_loop(0, count, tally, 0)

        def running(i, carry):
            total = carry + start[i]
            start[i] = total
            return total

        lax.fori_loop(0, owners + 1, running, 0)

        def place(i, carry):
            slot = class_ref[i] // own
            where = start[slot]
            order[where] = i
            start[slot] = where + 1
            return carry

        lax.fori_loop(0, count, place, 0)

    end = start[owner]
    begin = jnp.where(owner == 0, 0, start[jnp.maximum(owner - 1, 0)])
    acc[...] = jnp.zeros_like(acc)
    weight_ref[...] = jnp.zeros_like(weight_ref)
    row = lax.broadcasted_iota(jnp.int32, weight_ref.shape[1:], 0)

    def total(values):
        return jnp.sum(jnp.sum(values, axis=0, keepdims=True), axis=1, keepdims=True)

    def body(i, carry):
        p = order[i]
        k = class_ref[p] - owner * own
        tile = tile_ref[p].astype(F32)
        image = refs_ref[0, :, k].reshape(tile_len, tile_len).astype(F32)
        power = total(tile * tile) * scale
        ref_power = total(image * image) * scale
        meet = total(tile * image) * scale
        score = meet / jnp.sqrt((power + EPSILON) * (ref_power + EPSILON))
        weight = 1.0 / (1.0 + jnp.exp(-tile_len * score))
        scaling = (weight / jnp.sqrt(power + EPSILON)).astype(BF16).astype(F32)
        acc[k] += scaling * tile
        weight_ref[0] += jnp.where(row == k, weight, 0.0)
        return carry

    lax.fori_loop(begin, end, body, 0)
    for k in range(own):
        whole = acc[k].astype(BF16).reshape(reps, rows, tile_len)
        for rep in range(reps):
            sum_ref[0, rep % lanes, rep // lanes, k] = whole[rep]


def weigh(filtered, classes, refs, lanes):
    count, tile_len, _ = filtered.shape
    owners, reps, own, rows, _ = refs.shape
    slots = -(-own // 8) * 8
    block = (1, reps, own, rows, tile_len)
    parted = (owners, lanes, reps // lanes, own, rows, tile_len)
    grid_spec = pltpu.PrefetchScalarGridSpec(
        num_scalar_prefetch=1,
        grid=(owners,),
        in_specs=[
            pl.BlockSpec(filtered.shape, lambda o, *_: (0, 0, 0)),
            pl.BlockSpec(block, lambda o, *_: (o, 0, 0, 0, 0)),
        ],
        out_specs=[
            pl.BlockSpec((1,) + parted[1:], lambda o, *_: (o, 0, 0, 0, 0, 0)),
            pl.BlockSpec((1, slots, 128), lambda o, *_: (o, 0, 0)),
        ],
        scratch_shapes=[
            pltpu.VMEM((own, tile_len, tile_len), F32),
            pltpu.SMEM((owners + 1,), jnp.int32),
            pltpu.SMEM((count,), jnp.int32),
        ],
    )
    return pl.pallas_call(
        weigh_kernel,
        grid_spec=grid_spec,
        out_shape=[
            jax.ShapeDtypeStruct(parted, BF16),
            jax.ShapeDtypeStruct((owners, slots, 128), F32),
        ],
        compiler_params=pltpu.CompilerParams(vmem_limit_bytes=32 * MIB),
        name="weigh_tiles",
    )(classes, filtered, refs)


def reduce_kernel(
    sum_ref, weight_ref, own_ref, out_ref, near, far, share, deep, w_near, w_far, w_share, w_deep,
    near_sem, far_send, far_recv, deep_send, deep_recv, wn_sem, wf_send, wf_recv, wd_send, wd_recv
):
    owners, lanes, chips, own, rows, _ = sum_ref.shape
    me_z = lax.axis_index("cls")
    rep = lax.axis_index("rep")
    me_x, lane = rep // lanes, rep % lanes
    twin = {"rep": me_x * lanes + (1 - lane)}
    peers_x = [(me_x + d) % chips for d in range(1, chips)]
    peers_z = [(me_z + d) % owners for d in range(1, owners)]

    def copy(src, dst, send, recv, device):
        return pltpu.make_async_remote_copy(
            src_ref=src,
            dst_ref=dst,
            send_sem=send,
            recv_sem=recv,
            device_id=device,
            device_id_type=pl.DeviceIdType.MESH,
        )

    def to_x(x):
        return {"rep": x * lanes + lane}

    barrier = pltpu.get_barrier_semaphore()
    for device in [twin] + [to_x(x) for x in peers_x] + [{"cls": z} for z in peers_z]:
        pl.semaphore_signal(
            barrier, inc=1, device_id=device, device_id_type=pl.DeviceIdType.MESH
        )
    pl.semaphore_wait(barrier, chips + owners - 1)

    sends = []

    def launch(made):
        made.start()
        sends.append(made)

    order = peers_z + [me_z]
    launch(copy(weight_ref, w_near, wn_sem.at[0], wn_sem.at[1], twin))
    for o in order:
        launch(copy(sum_ref.at[o, 1 - lane], near.at[o], near_sem.at[0, o], near_sem.at[1, o], twin))

    copy(weight_ref, w_near, wn_sem.at[0], wn_sem.at[1], twin).wait_recv()
    w_share[...] = weight_ref[...] + w_near[...]
    for x in peers_x:
        launch(copy(w_share, w_far.at[me_x], wf_send.at[x], wf_recv.at[me_x], to_x(x)))
    for o in order:
        copy(
            sum_ref.at[o, lane], near.at[o], near_sem.at[0, o], near_sem.at[1, o], twin
        ).wait_recv()
        near[o] = (near[o].astype(F32) + sum_ref[o, lane].astype(F32)).astype(BF16)
        for x in peers_x:
            launch(
                copy(near.at[o, x], far.at[me_x, o], far_send.at[x, o], far_recv.at[me_x, o], to_x(x))
            )
    w_total = w_share[...]
    for x in peers_x:
        copy(w_share, w_far.at[x], wf_send.at[x], wf_recv.at[x], to_x(x)).wait_recv()
        w_total = w_total + w_far[x]
    for x in peers_x:
        made = copy(w_share, w_far.at[me_x], wf_send.at[x], wf_recv.at[me_x], to_x(x))
        made.wait_send()
        sends.pop(1 + owners)
    w_share[...] = w_total
    for z in peers_z:
        launch(copy(w_share.at[z], w_deep.at[me_z], wd_send.at[z], wd_recv.at[me_z], {"cls": z}))
    for o in order:
        total = near[o, me_x].astype(F32)
        for x in peers_x:
            copy(near.at[o, x], far.at[x, o], far_send.at[x, o], far_recv.at[x, o], to_x(x)).wait_recv()
            total = total + far[x, o].astype(F32)
        share[o] = total.astype(BF16)
        if o is not me_z:
            launch(copy(share.at[o], deep.at[me_z], deep_send.at[o], deep_recv.at[me_z], {"cls": o}))
    w_mine = w_share[me_z]
    for z in peers_z:
        copy(w_share.at[z], w_deep.at[z], wd_send.at[z], wd_recv.at[z], {"cls": z}).wait_recv()
        w_mine = w_mine + w_deep[z]
    for z in peers_z:
        copy(share.at[z], deep.at[z], deep_send.at[z], deep_recv.at[z], {"cls": z}).wait_recv()
    for k in range(own):
        total = PRIOR_WEIGHT * own_ref[k].astype(F32) + share[me_z, k].astype(F32)
        for z in peers_z:
            total = total + deep[z, k].astype(F32)
        out_ref[k] = total / (PRIOR_WEIGHT + w_mine[k : k + 1, 0:1])
    for made in sends:
        made.wait_send()


def reduce_update(sums, weights, references):
    owners, lanes, chips, own, rows, tile_len = sums.shape
    slots = weights.shape[1:]
    piece = (own, rows, tile_len)
    dma = pltpu.SemaphoreType.DMA
    return pl.pallas_call(
        reduce_kernel,
        out_shape=jax.ShapeDtypeStruct(references.shape, F32),
        in_specs=[pl.BlockSpec(memory_space=pltpu.VMEM)] * 3,
        out_specs=pl.BlockSpec(memory_space=pltpu.VMEM),
        scratch_shapes=[
            pltpu.VMEM((owners, chips) + piece, BF16),
            pltpu.VMEM((chips, owners) + piece, BF16),
            pltpu.VMEM((owners,) + piece, BF16),
            pltpu.VMEM((owners,) + piece, BF16),
            pltpu.VMEM((owners,) + slots, F32),
            pltpu.VMEM((chips, owners) + slots, F32),
            pltpu.VMEM((owners,) + slots, F32),
            pltpu.VMEM((owners,) + slots, F32),
            dma((2, owners)),
            dma((chips, owners)),
            dma((chips, owners)),
            dma((owners,)),
            dma((owners,)),
            dma((2,)),
            dma((chips,)),
            dma((chips,)),
            dma((owners,)),
            dma((owners,)),
        ],
        compiler_params=pltpu.CompilerParams(
            collective_id=1, has_side_effects=True, vmem_limit_bytes=32 * MIB
        ),
        name="reduce_update",
    )(sums, weights, references)


def local(particles, classes, rotation, defocus, filter_taps, ctf_table, references):
    owners = lax.axis_size("cls")
    reps = lax.axis_size("rep")
    own, rows, tile_len = references.shape
    refs = lax.all_gather(references, ("cls", "rep"), axis=0, tiled=False)
    refs = refs.reshape(owners, reps, own, rows, tile_len)
    filtered = filter_tiles(particles, rotation, defocus, filter_taps, ctf_table)
    small = reps % 2 == 0 and refs.size <= 4 * MIB
    sums, weights = weigh(filtered, classes, refs, 2 if small else 1)
    if small:
        return reduce_update(sums, weights, references)
    sums = sums.reshape(refs.shape)
    sums = lax.psum_scatter(sums, "rep", scatter_dimension=1, tiled=False)
    sums = lax.psum_scatter(sums, "cls", scatter_dimension=0, tiled=False)
    weights = lax.psum(weights[:, :own, 0], ("cls", "rep"))
    total = lax.dynamic_index_in_dim(weights, lax.axis_index("cls"), 0, keepdims=False)
    return (PRIOR_WEIGHT * references.astype(F32) + sums.astype(F32)) / (
        PRIOR_WEIGHT + total[:, None, None]
    )


def solution(mesh):
    placed = (
        P(("groups", "cls", "rep"), None, None),
        P(("groups", "cls", "rep")),
        P(("groups", "cls", "rep")),
        P(("groups", "cls", "rep")),
        P(),
        P(),
        P(("groups", "cls"), "rep", None),
    )
    return jax.shard_map(
        local,
        mesh=mesh,
        in_specs=placed,
        out_specs=P(("groups", "cls"), "rep", None),
        check_vma=False,
    )
```

```python
import functools
import math

import numpy as np

import jax
import jax.numpy as jnp
from jax import lax
from jax.experimental import pallas as pl
from jax.experimental.pallas import tpu as pltpu
from jax.sharding import PartitionSpec as P

EPSILON = 1e-05
PRIOR_WEIGHT = 4.0
F32 = jnp.float32
BF16 = jnp.bfloat16
MIB = 1 << 20


def hartley_table(tile_len):
    index = np.arange(tile_len, dtype=np.int64)
    phases = 2.0 * np.pi / tile_len * (index[:, None] * index[None, :] % tile_len)
    return (np.cos(phases) + np.sin(phases)).astype(np.float32)


def remote(src, dst, send, recv, device):
    return pltpu.make_async_remote_copy(
        src_ref=src,
        dst_ref=dst,
        send_sem=send,
        recv_sem=recv,
        device_id=device,
        device_id_type=pl.DeviceIdType.MESH,
    )


def enter(devices):
    barrier = pltpu.get_barrier_semaphore()
    for device in devices:
        pl.semaphore_signal(
            barrier, inc=1, device_id=device, device_id_type=pl.DeviceIdType.MESH
        )
    pl.semaphore_wait(barrier, len(devices))


def gather_steps(own_ref, all_ref, sems):
    keep, z_send, z_recv, x_send, x_recv, t_send, t_recv = sems
    owners, lanes, chips = all_ref.shape[:3]
    me_z = lax.axis_index("cls")
    rep = lax.axis_index("rep")
    me_x, lane = rep // lanes, rep % lanes
    twin = {"rep": me_x * lanes + (1 - lane)}
    next_x = [(me_x + d) % chips for d in range(1, chips)]
    from_z = [(me_z + owners - d) % owners for d in range(1, owners)]
    to_z = [(me_z + d) % owners for d in range(1, owners)]
    held = all_ref.at[me_z, lane, me_x]

    def to_x(x):
        return {"rep": x * lanes + lane}

    def across_z(z, slot):
        return remote(own_ref, all_ref.at[slot, lane, me_x], z_send.at[z], z_recv.at[slot], {"cls": z})

    def across_x(src, x, z, slot):
        return remote(src, all_ref.at[z, lane, slot], x_send.at[x, z], x_recv.at[slot, z], to_x(x))

    def across_twin(src, z, x):
        return remote(src, all_ref.at[z, lane, x], t_send.at[x, z], t_recv.at[x, z], twin)

    def begin():
        enter([twin] + [to_x(x) for x in next_x] + [{"cls": z} for z in to_z])
        pltpu.make_async_copy(own_ref, held, keep).start()
        for z in to_z:
            across_z(z, me_z).start()
        for x in next_x:
            across_x(own_ref, x, me_z, me_x).start()
        across_twin(own_ref, me_z, me_x).start()

    def pass_z(z):
        across_z(z, z).wait_recv()
        src = all_ref.at[z, lane, me_x]
        for x in next_x:
            across_x(src, x, z, me_x).start()
        across_twin(src, z, me_x).start()

    def pass_x(z):
        for x in next_x:
            across_x(own_ref, x, z, x).wait_recv()
            across_twin(all_ref.at[z, lane, x], z, x).start()

    def finish():
        pltpu.make_async_copy(own_ref, held, keep).wait()
        for z in [me_z] + from_z:
            for x in [me_x] + next_x:
                remote(
                    own_ref, all_ref.at[z, 1 - lane, x], t_send.at[x, z], t_recv.at[x, z], twin
                ).wait()
            for x in next_x:
                across_x(own_ref, x, z, me_x).wait_send()
        for z in to_z:
            across_z(z, me_z).wait_send()

    stages = [begin]
    for d, z in enumerate(from_z):
        stages.append(functools.partial(pass_z, z))
        stages.append(functools.partial(pass_x, me_z if d == 0 else from_z[d - 1]))
    stages.append(functools.partial(pass_x, from_z[-1]))
    stages.append(finish)
    return stages


def filter_kernel(
    turn_ref, bin_ref, taps_ref, hartley_ref, ctf_ref, tile_ref, *rest
):
    if len(rest) > 4:
        own_ref, out_ref, all_ref, fwd, fwd_t, syn = rest[:6]
        stages = gather_steps(own_ref, all_ref, rest[6:])
    else:
        out_ref, fwd, fwd_t, syn = rest
        stages = []
    batch, tile_len, _ = tile_ref.shape
    taps = taps_ref.shape[0]
    half = (taps - 1) // 2
    step = pl.program_id(0)
    steps = pl.num_programs(0)

    @pl.when(step == 0)
    def _():
        if stages:
            stages[0]()
        row = lax.broadcasted_iota(jnp.int32, (tile_len, tile_len), 0)
        col = lax.broadcasted_iota(jnp.int32, (tile_len, tile_len), 1)
        gap = col - row
        band = jnp.zeros((tile_len, tile_len), F32)
        for tap in range(taps):
            band = jnp.where(gap == tap - half, taps_ref[tap], band)
        hartley = hartley_ref[...]
        analysis = jnp.dot(
            hartley, band, preferred_element_type=F32, precision=lax.Precision.HIGHEST
        ).astype(BF16)
        mirror = jnp.where(row + col == tile_len - 1, 1.0, 0.0).astype(BF16)
        mirrored = jnp.dot(analysis, mirror, preferred_element_type=F32)
        fwd[0] = analysis
        fwd[1] = mirrored.astype(BF16)
        fwd_t[0] = analysis.astype(F32).T.astype(BF16)
        fwd_t[1] = mirrored.T.astype(BF16)
        syn[...] = hartley.astype(BF16)

    for i in range(batch):
        code = turn_ref[step * batch + i]
        tile = tile_ref[i]
        tile = jnp.where(code >= 4, tile.T, tile)
        first = jnp.dot(tile, fwd_t[(code // 2) % 2], preferred_element_type=F32).astype(BF16)
        raw = jnp.dot(fwd[code % 2], first, preferred_element_type=F32)
        gain = ctf_ref[bin_ref[step * batch + i]].astype(F32)
        spectra = (raw * gain).astype(BF16)
        second = jnp.dot(spectra, syn[...], preferred_element_type=F32).astype(BF16)
        result = jnp.dot(syn[...], second, preferred_element_type=F32)
        out_ref[i] = (result * (1.0 / (tile_len * tile_len))).astype(BF16)

    for at, stage in enumerate(stages[1:]):

        @pl.when(step == jnp.minimum(at + 1, steps - 1))
        def _(stage=stage):
            stage()


def filter_tiles(particles, rotation, defocus, filter_taps, ctf_table, references, gather):
    count, tile_len, _ = particles.shape
    batch = math.gcd(count, 4)
    hartley = jnp.asarray(hartley_table(tile_len))
    square = (tile_len, tile_len)
    in_specs = [pl.BlockSpec(memory_space=pltpu.SMEM)] * 3 + [
        pl.BlockSpec(square, lambda i: (0, 0)),
        pl.BlockSpec(ctf_table.shape, lambda i: (0, 0, 0)),
        pl.BlockSpec((batch,) + square, lambda i: (i, 0, 0)),
    ]
    out_specs = [pl.BlockSpec((batch,) + square, lambda i: (i, 0, 0))]
    out_shape = [jax.ShapeDtypeStruct(particles.shape, BF16)]
    scratch = [
        pltpu.VMEM((2,) + square, BF16),
        pltpu.VMEM((2,) + square, BF16),
        pltpu.VMEM(square, BF16),
    ]
    operands = [rotation, defocus, filter_taps, hartley, ctf_table, particles]
    params = dict(vmem_limit_bytes=56 * MIB)
    if gather:
        owners, lanes, chips = gather
        dma = pltpu.SemaphoreType.DMA
        in_specs.append(pl.BlockSpec(memory_space=pl.ANY))
        out_specs.append(pl.BlockSpec(memory_space=pl.ANY))
        out_shape.append(jax.ShapeDtypeStruct(gather + references.shape, BF16))
        scratch += [
            dma,
            dma((owners,)),
            dma((owners,)),
            dma((chips, owners)),
            dma((chips, owners)),
            dma((chips, owners)),
            dma((chips, owners)),
        ]
        operands.append(references)
        params.update(collective_id=2, has_side_effects=True)
    return pl.pallas_call(
        filter_kernel,
        grid=(count // batch,),
        in_specs=in_specs,
        out_specs=out_specs,
        scratch_shapes=scratch,
        out_shape=out_shape,
        compiler_params=pltpu.CompilerParams(**params),
        cost_estimate=pl.CostEstimate(
            flops=8 * count * tile_len**3,
            bytes_accessed=4 * count * tile_len**2,
            transcendentals=0,
        ),
        name="filter_tiles",
    )(*operands)


def weigh_kernel(class_ref, tile_ref, refs_ref, sum_ref, weight_ref, acc, start, order):
    count, tile_len, _ = tile_ref.shape
    _, lanes, chips, own, rows, _ = refs_ref.shape
    reps = lanes * chips
    owners = pl.num_programs(0)
    owner = pl.program_id(0)
    scale = 1.0 / (tile_len * tile_len)

    @pl.when(owner == 0)
    def _():
        def clear(i, carry):
            start[i] = 0
            return carry

        lax.fori_loop(0, owners + 1, clear, 0)

        def tally(i, carry):
            slot = class_ref[i] // own + 1
            start[slot] = start[slot] + 1
            return carry

        lax.fori_loop(0, count, tally, 0)

        def running(i, carry):
            total = carry + start[i]
            start[i] = total
            return total

        lax.fori_loop(0, owners + 1, running, 0)

        def place(i, carry):
            slot = class_ref[i] // own
            where = start[slot]
            order[where] = i
            start[slot] = where + 1
            return carry

        lax.fori_loop(0, count, place, 0)

    end = start[owner]
    begin = jnp.where(owner == 0, 0, start[jnp.maximum(owner - 1, 0)])
    acc[...] = jnp.zeros_like(acc)
    weight_ref[...] = jnp.zeros_like(weight_ref)
    row = lax.broadcasted_iota(jnp.int32, weight_ref.shape[1:], 0)

    def total(values):
        return jnp.sum(jnp.sum(values, axis=0, keepdims=True), axis=1, keepdims=True)

    def body(i, carry):
        p = order[i]
        k = class_ref[p] - owner * own
        tile = tile_ref[p].astype(F32)
        image = jnp.concatenate(
            [refs_ref[0, rep % lanes, rep // lanes, k] for rep in range(reps)], axis=0
        ).astype(F32)
        power = total(tile * tile) * scale
        ref_power = total(image * image) * scale
        meet = total(tile * image) * scale
        score = meet / jnp.sqrt((power + EPSILON) * (ref_power + EPSILON))
        weight = 1.0 / (1.0 + jnp.exp(-tile_len * score))
        scaling = (weight / jnp.sqrt(power + EPSILON)).astype(BF16).astype(F32)
        acc[k] += scaling * tile
        weight_ref[0] += jnp.where(row == k, weight, 0.0)
        return carry

    lax.fori_loop(begin, end, body, 0)
    for k in range(own):
        whole = acc[k].astype(BF16).reshape(reps, rows, tile_len)
        for rep in range(reps):
            sum_ref[0, rep % lanes, rep // lanes, k] = whole[rep]


def weigh(filtered, classes, refs):
    count, tile_len, _ = filtered.shape
    owners, lanes, chips, own, rows, _ = refs.shape
    slots = -(-own // 8) * 8
    block = (1,) + refs.shape[1:]
    grid_spec = pltpu.PrefetchScalarGridSpec(
        num_scalar_prefetch=1,
        grid=(owners,),
        in_specs=[
            pl.BlockSpec(filtered.shape, lambda o, *_: (0, 0, 0)),
            pl.BlockSpec(block, lambda o, *_: (o, 0, 0, 0, 0, 0)),
        ],
        out_specs=[
            pl.BlockSpec(block, lambda o, *_: (o, 0, 0, 0, 0, 0)),
            pl.BlockSpec((1, slots, 128), lambda o, *_: (o, 0, 0)),
        ],
        scratch_shapes=[
            pltpu.VMEM((own, tile_len, tile_len), F32),
            pltpu.SMEM((owners + 1,), jnp.int32),
            pltpu.SMEM((count,), jnp.int32),
        ],
    )
    return pl.pallas_call(
        weigh_kernel,
        grid_spec=grid_spec,
        out_shape=[
            jax.ShapeDtypeStruct(refs.shape, BF16),
            jax.ShapeDtypeStruct((owners, slots, 128), F32),
        ],
        compiler_params=pltpu.CompilerParams(vmem_limit_bytes=56 * MIB),
        name="weigh_tiles",
    )(classes, filtered, refs)


def reduce_kernel(
    sum_ref, weight_ref, own_ref, out_ref, near, far, share, deep, w_near, w_far, w_share, w_deep,
    near_sem, far_send, far_recv, deep_send, deep_recv, wn_sem, wf_send, wf_recv, wd_send, wd_recv
):
    owners, lanes, chips, own, rows, _ = sum_ref.shape
    me_z = lax.axis_index("cls")
    rep = lax.axis_index("rep")
    me_x, lane = rep // lanes, rep % lanes
    twin = {"rep": me_x * lanes + (1 - lane)}
    peers_x = [(me_x + d) % chips for d in range(1, chips)]
    peers_z = [(me_z + d) % owners for d in range(1, owners)]

    def copy(src, dst, send, recv, device):
        return pltpu.make_async_remote_copy(
            src_ref=src,
            dst_ref=dst,
            send_sem=send,
            recv_sem=recv,
            device_id=device,
            device_id_type=pl.DeviceIdType.MESH,
        )

    def to_x(x):
        return {"rep": x * lanes + lane}

    barrier = pltpu.get_barrier_semaphore()
    for device in [twin] + [to_x(x) for x in peers_x] + [{"cls": z} for z in peers_z]:
        pl.semaphore_signal(
            barrier, inc=1, device_id=device, device_id_type=pl.DeviceIdType.MESH
        )
    pl.semaphore_wait(barrier, chips + owners - 1)

    sends = []

    def launch(made):
        made.start()
        sends.append(made)

    order = peers_z + [me_z]
    launch(copy(weight_ref, w_near, wn_sem.at[0], wn_sem.at[1], twin))
    for o in order:
        launch(copy(sum_ref.at[o, 1 - lane], near.at[o], near_sem.at[0, o], near_sem.at[1, o], twin))

    copy(weight_ref, w_near, wn_sem.at[0], wn_sem.at[1], twin).wait_recv()
    w_share[...] = weight_ref[...] + w_near[...]
    for x in peers_x:
        launch(copy(w_share, w_far.at[me_x], wf_send.at[x], wf_recv.at[me_x], to_x(x)))
    for o in order:
        copy(
            sum_ref.at[o, lane], near.at[o], near_sem.at[0, o], near_sem.at[1, o], twin
        ).wait_recv()
        near[o] = (near[o].astype(F32) + sum_ref[o, lane].astype(F32)).astype(BF16)
        for x in peers_x:
            launch(
                copy(near.at[o, x], far.at[me_x, o], far_send.at[x, o], far_recv.at[me_x, o], to_x(x))
            )
    w_total = w_share[...]
    for x in peers_x:
        copy(w_share, w_far.at[x], wf_send.at[x], wf_recv.at[x], to_x(x)).wait_recv()
        w_total = w_total + w_far[x]
    for x in peers_x:
        made = copy(w_share, w_far.at[me_x], wf_send.at[x], wf_recv.at[me_x], to_x(x))
        made.wait_send()
        sends.pop(1 + owners)
    w_share[...] = w_total
    for z in peers_z:
        launch(copy(w_share.at[z], w_deep.at[me_z], wd_send.at[z], wd_recv.at[me_z], {"cls": z}))
    for o in order:
        total = near[o, me_x].astype(F32)
        for x in peers_x:
            copy(near.at[o, x], far.at[x, o], far_send.at[x, o], far_recv.at[x, o], to_x(x)).wait_recv()
            total = total + far[x, o].astype(F32)
        share[o] = total.astype(BF16)
        if o is not me_z:
            launch(copy(share.at[o], deep.at[me_z], deep_send.at[o], deep_recv.at[me_z], {"cls": o}))
    w_mine = w_share[me_z]
    for z in peers_z:
        copy(w_share.at[z], w_deep.at[z], wd_send.at[z], wd_recv.at[z], {"cls": z}).wait_recv()
        w_mine = w_mine + w_deep[z]
    for z in peers_z:
        copy(share.at[z], deep.at[z], deep_send.at[z], deep_recv.at[z], {"cls": z}).wait_recv()
    for k in range(own):
        total = PRIOR_WEIGHT * own_ref[k].astype(F32) + share[me_z, k].astype(F32)
        for z in peers_z:
            total = total + deep[z, k].astype(F32)
        out_ref[k] = total / (PRIOR_WEIGHT + w_mine[k : k + 1, 0:1])
    for made in sends:
        made.wait_send()


def reduce_update(sums, weights, references):
    owners, lanes, chips, own, rows, tile_len = sums.shape
    slots = weights.shape[1:]
    piece = (own, rows, tile_len)
    dma = pltpu.SemaphoreType.DMA
    return pl.pallas_call(
        reduce_kernel,
        out_shape=jax.ShapeDtypeStruct(references.shape, F32),
        in_specs=[pl.BlockSpec(memory_space=pltpu.VMEM)] * 3,
        out_specs=pl.BlockSpec(memory_space=pltpu.VMEM),
        scratch_shapes=[
            pltpu.VMEM((owners, chips) + piece, BF16),
            pltpu.VMEM((chips, owners) + piece, BF16),
            pltpu.VMEM((owners,) + piece, BF16),
            pltpu.VMEM((owners,) + piece, BF16),
            pltpu.VMEM((owners,) + slots, F32),
            pltpu.VMEM((chips, owners) + slots, F32),
            pltpu.VMEM((owners,) + slots, F32),
            pltpu.VMEM((owners,) + slots, F32),
            dma((2, owners)),
            dma((chips, owners)),
            dma((chips, owners)),
            dma((owners,)),
            dma((owners,)),
            dma((2,)),
            dma((chips,)),
            dma((chips,)),
            dma((owners,)),
            dma((owners,)),
        ],
        compiler_params=pltpu.CompilerParams(
            collective_id=1, has_side_effects=True, vmem_limit_bytes=32 * MIB
        ),
        name="reduce_update",
    )(sums, weights, references)


def local(particles, classes, rotation, defocus, filter_taps, ctf_table, references):
    owners = lax.axis_size("cls")
    reps = lax.axis_size("rep")
    own, rows, tile_len = references.shape
    stack = (owners, 2, reps // 2)
    small = reps % 2 == 0 and owners * reps * references.size <= 4 * MIB
    tiles = (particles, rotation, defocus, filter_taps, ctf_table, references)
    if small:
        filtered, refs = filter_tiles(*tiles, stack)
        sums, weights = weigh(filtered, classes, refs)
        return reduce_update(sums, weights, references)
    refs = lax.all_gather(references, ("cls", "rep"), axis=0, tiled=False)
    [filtered] = filter_tiles(*tiles, None)
    refs = refs.reshape(owners, 1, reps, own, rows, tile_len)
    sums, weights = weigh(filtered, classes, refs)
    sums = sums[:, 0]
    sums = lax.psum_scatter(sums, "rep", scatter_dimension=1, tiled=False)
    sums = lax.psum_scatter(sums, "cls", scatter_dimension=0, tiled=False)
    weights = lax.psum(weights[:, :own, 0], ("cls", "rep"))
    total = lax.dynamic_index_in_dim(weights, lax.axis_index("cls"), 0, keepdims=False)
    return (PRIOR_WEIGHT * references.astype(F32) + sums.astype(F32)) / (
        PRIOR_WEIGHT + total[:, None, None]
    )


def solution(mesh):
    placed = (
        P(("groups", "cls", "rep"), None, None),
        P(("groups", "cls", "rep")),
        P(("groups", "cls", "rep")),
        P(("groups", "cls", "rep")),
        P(),
        P(),
        P(("groups", "cls"), "rep", None),
    )
    return jax.shard_map(
        local,
        mesh=mesh,
        in_specs=placed,
        out_specs=P(("groups", "cls"), "rep", None),
        check_vma=False,
    )
```

```python
import functools
import math

import numpy as np

import jax
import jax.numpy as jnp
from jax import lax
from jax.experimental import pallas as pl
from jax.experimental.pallas import tpu as pltpu
from jax.sharding import PartitionSpec as P

EPSILON = 1e-05
PRIOR_WEIGHT = 4.0
F32 = jnp.float32
BF16 = jnp.bfloat16
MIB = 1 << 20


def hartley_table(tile_len):
    index = np.arange(tile_len, dtype=np.int64)
    phases = 2.0 * np.pi / tile_len * (index[:, None] * index[None, :] % tile_len)
    return (np.cos(phases) + np.sin(phases)).astype(np.float32)


def remote(src, dst, send, recv, device):
    return pltpu.make_async_remote_copy(
        src_ref=src,
        dst_ref=dst,
        send_sem=send,
        recv_sem=recv,
        device_id=device,
        device_id_type=pl.DeviceIdType.MESH,
    )


def enter(devices):
    barrier = pltpu.get_barrier_semaphore()
    for device in devices:
        pl.semaphore_signal(
            barrier, inc=1, device_id=device, device_id_type=pl.DeviceIdType.MESH
        )
    pl.semaphore_wait(barrier, len(devices))


def gather_steps(own_ref, all_ref, sems):
    keep, z_send, z_recv, x_send, x_recv, t_send, t_recv = sems
    owners, lanes, chips = all_ref.shape[:3]
    me_z = lax.axis_index("cls")
    rep = lax.axis_index("rep")
    me_x, lane = rep // lanes, rep % lanes
    twin = {"rep": me_x * lanes + (1 - lane)}
    next_x = [(me_x + d) % chips for d in range(1, chips)]
    held = all_ref.at[me_z, lane, me_x]
    has_left, has_right = me_z > 0, me_z < owners - 1

    def to_x(x):
        return {"rep": x * lanes + lane}

    def along_z(src, z, way):
        return remote(
            src,
            all_ref.at[z, lane, me_x],
            z_send.at[way, z],
            z_recv.at[z],
            {"cls": me_z + 1 if way else me_z - 1},
        )

    def across_x(src, x, z, slot):
        return remote(src, all_ref.at[z, lane, slot], x_send.at[x, z], x_recv.at[slot, z], to_x(x))

    def across_twin(src, z, x):
        return remote(src, all_ref.at[z, lane, x], t_send.at[x, z], t_recv.at[x, z], twin)

    def begin():
        others = [{"cls": (me_z + d) % owners} for d in range(1, owners)]
        enter([twin] + [to_x(x) for x in next_x] + others)
        pl.when(has_right)(lambda: along_z(own_ref, me_z, 1).start())
        pl.when(has_left)(lambda: along_z(own_ref, me_z, 0).start())
        for x in next_x:
            across_x(own_ref, x, me_z, me_x).start()
        across_twin(own_ref, me_z, me_x).start()
        pltpu.make_async_copy(own_ref, held, keep).start()

    def sides(distance):
        low, high = me_z - distance, me_z + distance
        return [(low >= 0, low, has_right, 1), (high < owners, high, has_left, 0)]

    def pass_z(distance):
        for there, z, onward, way in sides(distance):

            @pl.when(there)
            def _(z=z, onward=onward, way=way):
                src = all_ref.at[z, lane, me_x]
                along_z(own_ref, z, way).wait_recv()
                pl.when(onward)(lambda: along_z(src, z, way).start())
                for x in next_x:
                    across_x(src, x, z, me_x).start()
                across_twin(src, z, me_x).start()

    def pass_x(z):
        for x in next_x:
            across_x(own_ref, x, z, x).wait_recv()
            across_twin(all_ref.at[z, lane, x], z, x).start()

    def pass_x_side(distance, side):
        there, z, _, _ = sides(distance)[side]
        pl.when(there)(lambda: pass_x(z))

    def finish():
        pltpu.make_async_copy(own_ref, held, keep).wait()
        for z in range(owners):
            for x in [me_x] + next_x:
                remote(
                    own_ref, all_ref.at[z, 1 - lane, x], t_send.at[x, z], t_recv.at[x, z], twin
                ).wait()
            for x in next_x:
                across_x(own_ref, x, z, me_x).wait_send()
        pl.when(has_right)(lambda: along_z(own_ref, me_z, 1).wait_send())
        pl.when(has_left)(lambda: along_z(own_ref, me_z, 0).wait_send())
        for distance in range(1, owners):
            for there, z, onward, way in sides(distance):
                pl.when(there & onward)(
                    functools.partial(lambda z, way: along_z(own_ref, z, way).wait_send(), z, way)
                )

    stages = [(0, begin), (5, functools.partial(pass_x, me_z))]
    for d in range(1, owners):
        stages.append((4 * d, functools.partial(pass_z, d)))
        stages.append((4 * d + 5, functools.partial(pass_x_side, d, 0)))
        stages.append((4 * d + 7, functools.partial(pass_x_side, d, 1)))
    stages.sort(key=lambda entry: entry[0])
    return stages + [(1 << 20, finish)]


def filter_kernel(
    turn_ref, bin_ref, taps_ref, hartley_ref, ctf_ref, tile_ref, *rest
):
    if len(rest) > 4:
        own_ref, out_ref, all_ref, fwd, fwd_t, syn = rest[:6]
        stages = gather_steps(own_ref, all_ref, rest[6:])
    else:
        out_ref, fwd, fwd_t, syn = rest
        stages = []
    batch, tile_len, _ = tile_ref.shape
    taps = taps_ref.shape[0]
    half = (taps - 1) // 2
    step = pl.program_id(0)
    steps = pl.num_programs(0)

    @pl.when(step == 0)
    def _():
        if stages:
            stages[0][1]()
        row = lax.broadcasted_iota(jnp.int32, (tile_len, tile_len), 0)
        col = lax.broadcasted_iota(jnp.int32, (tile_len, tile_len), 1)
        gap = col - row
        band = jnp.zeros((tile_len, tile_len), F32)
        for tap in range(taps):
            band = jnp.where(gap == tap - half, taps_ref[tap], band)
        hartley = hartley_ref[...]
        analysis = jnp.dot(
            hartley, band, preferred_element_type=F32, precision=lax.Precision.HIGHEST
        ).astype(BF16)
        mirror = jnp.where(row + col == tile_len - 1, 1.0, 0.0).astype(BF16)
        mirrored = jnp.dot(analysis, mirror, preferred_element_type=F32)
        fwd[0] = analysis
        fwd[1] = mirrored.astype(BF16)
        fwd_t[0] = analysis.astype(F32).T.astype(BF16)
        fwd_t[1] = mirrored.T.astype(BF16)
        syn[...] = hartley.astype(BF16)

    for i in range(batch):
        code = turn_ref[step * batch + i]
        tile = tile_ref[i]
        tile = jnp.where(code >= 4, tile.T, tile)
        first = jnp.dot(tile, fwd_t[(code // 2) % 2], preferred_element_type=F32).astype(BF16)
        raw = jnp.dot(fwd[code % 2], first, preferred_element_type=F32)
        gain = ctf_ref[bin_ref[step * batch + i]].astype(F32)
        spectra = (raw * gain).astype(BF16)
        second = jnp.dot(spectra, syn[...], preferred_element_type=F32).astype(BF16)
        result = jnp.dot(syn[...], second, preferred_element_type=F32)
        out_ref[i] = (result * (1.0 / (tile_len * tile_len))).astype(BF16)

    for at, stage in stages[1:]:

        @pl.when(step == jnp.minimum(at, steps - 1))
        def _(stage=stage):
            stage()


def filter_tiles(particles, rotation, defocus, filter_taps, ctf_table, references, gather):
    count, tile_len, _ = particles.shape
    batch = math.gcd(count, 2)
    hartley = jnp.asarray(hartley_table(tile_len))
    square = (tile_len, tile_len)
    in_specs = [pl.BlockSpec(memory_space=pltpu.SMEM)] * 3 + [
        pl.BlockSpec(square, lambda i: (0, 0)),
        pl.BlockSpec(ctf_table.shape, lambda i: (0, 0, 0)),
        pl.BlockSpec((batch,) + square, lambda i: (i, 0, 0)),
    ]
    out_specs = [pl.BlockSpec((batch,) + square, lambda i: (i, 0, 0))]
    out_shape = [jax.ShapeDtypeStruct(particles.shape, BF16)]
    scratch = [
        pltpu.VMEM((2,) + square, BF16),
        pltpu.VMEM((2,) + square, BF16),
        pltpu.VMEM(square, BF16),
    ]
    operands = [rotation, defocus, filter_taps, hartley, ctf_table, particles]
    params = dict(vmem_limit_bytes=56 * MIB)
    if gather:
        owners, lanes, chips = gather
        dma = pltpu.SemaphoreType.DMA
        in_specs.append(pl.BlockSpec(memory_space=pl.ANY))
        out_specs.append(pl.BlockSpec(memory_space=pl.ANY))
        out_shape.append(jax.ShapeDtypeStruct(gather + references.shape, BF16))
        scratch += [
            dma,
            dma((2, owners)),
            dma((owners,)),
            dma((chips, owners)),
            dma((chips, owners)),
            dma((chips, owners)),
            dma((chips, owners)),
        ]
        operands.append(references)
        params.update(collective_id=2, has_side_effects=True)
    return pl.pallas_call(
        filter_kernel,
        grid=(count // batch,),
        in_specs=in_specs,
        out_specs=out_specs,
        scratch_shapes=scratch,
        out_shape=out_shape,
        compiler_params=pltpu.CompilerParams(**params),
        cost_estimate=pl.CostEstimate(
            flops=8 * count * tile_len**3,
            bytes_accessed=4 * count * tile_len**2,
            transcendentals=0,
        ),
        name="filter_tiles",
    )(*operands)


def weigh_kernel(class_ref, tile_ref, refs_ref, sum_ref, weight_ref, acc, start, order):
    count, tile_len, _ = tile_ref.shape
    _, lanes, chips, own, rows, _ = refs_ref.shape
    reps = lanes * chips
    owners = pl.num_programs(0)
    owner = pl.program_id(0)
    scale = 1.0 / (tile_len * tile_len)

    @pl.when(owner == 0)
    def _():
        def clear(i, carry):
            start[i] = 0
            return carry

        lax.fori_loop(0, owners + 1, clear, 0)

        def tally(i, carry):
            slot = class_ref[i] // own + 1
            start[slot] = start[slot] + 1
            return carry

        lax.fori_loop(0, count, tally, 0)

        def running(i, carry):
            total = carry + start[i]
            start[i] = total
            return total

        lax.fori_loop(0, owners + 1, running, 0)

        def place(i, carry):
            slot = class_ref[i] // own
            where = start[slot]
            order[where] = i
            start[slot] = where + 1
            return carry

        lax.fori_loop(0, count, place, 0)

    end = start[owner]
    begin = jnp.where(owner == 0, 0, start[jnp.maximum(owner - 1, 0)])
    acc[...] = jnp.zeros_like(acc)
    weight_ref[...] = jnp.zeros_like(weight_ref)
    row = lax.broadcasted_iota(jnp.int32, weight_ref.shape[1:], 0)

    def total(values):
        return jnp.sum(jnp.sum(values, axis=0, keepdims=True), axis=1, keepdims=True)

    def body(i, carry):
        p = order[i]
        k = class_ref[p] - owner * own
        tile = tile_ref[p].astype(F32)
        image = jnp.concatenate(
            [refs_ref[0, rep % lanes, rep // lanes, k] for rep in range(reps)], axis=0
        ).astype(F32)
        power = total(tile * tile) * scale
        ref_power = total(image * image) * scale
        meet = total(tile * image) * scale
        score = meet / jnp.sqrt((power + EPSILON) * (ref_power + EPSILON))
        weight = 1.0 / (1.0 + jnp.exp(-tile_len * score))
        scaling = (weight / jnp.sqrt(power + EPSILON)).astype(BF16).astype(F32)
        acc[k] += scaling * tile
        weight_ref[0] += jnp.where(row == k, weight, 0.0)
        return carry

    lax.fori_loop(begin, end, body, 0)
    for k in range(own):
        whole = acc[k].astype(BF16).reshape(reps, rows, tile_len)
        for rep in range(reps):
            sum_ref[0, rep % lanes, rep // lanes, k] = whole[rep]


def weigh(filtered, classes, refs):
    count, tile_len, _ = filtered.shape
    owners, lanes, chips, own, rows, _ = refs.shape
    slots = -(-own // 8) * 8
    block = (1,) + refs.shape[1:]
    grid_spec = pltpu.PrefetchScalarGridSpec(
        num_scalar_prefetch=1,
        grid=(owners,),
        in_specs=[
            pl.BlockSpec(filtered.shape, lambda o, *_: (0, 0, 0)),
            pl.BlockSpec(block, lambda o, *_: (o, 0, 0, 0, 0, 0)),
        ],
        out_specs=[
            pl.BlockSpec(block, lambda o, *_: (o, 0, 0, 0, 0, 0)),
            pl.BlockSpec((1, slots, 128), lambda o, *_: (o, 0, 0)),
        ],
        scratch_shapes=[
            pltpu.VMEM((own, tile_len, tile_len), F32),
            pltpu.SMEM((owners + 1,), jnp.int32),
            pltpu.SMEM((count,), jnp.int32),
        ],
    )
    return pl.pallas_call(
        weigh_kernel,
        grid_spec=grid_spec,
        out_shape=[
            jax.ShapeDtypeStruct(refs.shape, BF16),
            jax.ShapeDtypeStruct((owners, slots, 128), F32),
        ],
        compiler_params=pltpu.CompilerParams(vmem_limit_bytes=56 * MIB),
        name="weigh_tiles",
    )(classes, filtered, refs)


def reduce_kernel(
    sum_ref, weight_ref, own_ref, out_ref, near, far, share, deep, w_near, w_far, w_share, w_deep,
    kept, keep, near_sem, far_send, far_recv, deep_send, deep_recv, wn_sem, wf_send, wf_recv, wd_send, wd_recv
):
    owners, lanes, chips, own, rows, _ = sum_ref.shape
    me_z = lax.axis_index("cls")
    rep = lax.axis_index("rep")
    me_x, lane = rep // lanes, rep % lanes
    twin = {"rep": me_x * lanes + (1 - lane)}
    peers_x = [(me_x + d) % chips for d in range(1, chips)]
    peers_z = [(me_z + d) % owners for d in range(1, owners)]

    def copy(src, dst, send, recv, device):
        return pltpu.make_async_remote_copy(
            src_ref=src,
            dst_ref=dst,
            send_sem=send,
            recv_sem=recv,
            device_id=device,
            device_id_type=pl.DeviceIdType.MESH,
        )

    def to_x(x):
        return {"rep": x * lanes + lane}

    barrier = pltpu.get_barrier_semaphore()
    for device in [twin] + [to_x(x) for x in peers_x] + [{"cls": z} for z in peers_z]:
        pl.semaphore_signal(
            barrier, inc=1, device_id=device, device_id_type=pl.DeviceIdType.MESH
        )
    pl.semaphore_wait(barrier, chips + owners - 1)

    sends = []

    def launch(made):
        made.start()
        sends.append(made)

    order = peers_z + [me_z]
    launch(copy(weight_ref, w_near, wn_sem.at[0], wn_sem.at[1], twin))
    for o in order:
        launch(copy(sum_ref.at[o, 1 - lane], near.at[o], near_sem.at[0, o], near_sem.at[1, o], twin))

    for o in order:
        pltpu.make_async_copy(sum_ref.at[o, lane], kept.at[o], keep.at[o]).start()
    copy(weight_ref, w_near, wn_sem.at[0], wn_sem.at[1], twin).wait_recv()
    w_share[...] = weight_ref[...] + w_near[...]
    for x in peers_x:
        launch(copy(w_share, w_far.at[me_x], wf_send.at[x], wf_recv.at[me_x], to_x(x)))
    for o in order:
        copy(
            sum_ref.at[o, lane], near.at[o], near_sem.at[0, o], near_sem.at[1, o], twin
        ).wait_recv()
        pltpu.make_async_copy(sum_ref.at[o, lane], kept.at[o], keep.at[o]).wait()
        near[o] = (near[o].astype(F32) + kept[o].astype(F32)).astype(BF16)
        for x in peers_x:
            launch(
                copy(near.at[o, x], far.at[me_x, o], far_send.at[x, o], far_recv.at[me_x, o], to_x(x))
            )
    w_total = w_share[...]
    for x in peers_x:
        copy(w_share, w_far.at[x], wf_send.at[x], wf_recv.at[x], to_x(x)).wait_recv()
        w_total = w_total + w_far[x]
    for x in peers_x:
        made = copy(w_share, w_far.at[me_x], wf_send.at[x], wf_recv.at[me_x], to_x(x))
        made.wait_send()
        sends.pop(1 + owners)
    w_share[...] = w_total
    for z in peers_z:
        launch(copy(w_share.at[z], w_deep.at[me_z], wd_send.at[z], wd_recv.at[me_z], {"cls": z}))
    for o in order:
        total = near[o, me_x].astype(F32)
        for x in peers_x:
            copy(near.at[o, x], far.at[x, o], far_send.at[x, o], far_recv.at[x, o], to_x(x)).wait_recv()
            total = total + far[x, o].astype(F32)
        share[o] = total.astype(BF16)
        if o is not me_z:
            launch(copy(share.at[o], deep.at[me_z], deep_send.at[o], deep_recv.at[me_z], {"cls": o}))
    w_mine = w_share[me_z]
    for z in peers_z:
        copy(w_share.at[z], w_deep.at[z], wd_send.at[z], wd_recv.at[z], {"cls": z}).wait_recv()
        w_mine = w_mine + w_deep[z]
    for z in peers_z:
        copy(share.at[z], deep.at[z], deep_send.at[z], deep_recv.at[z], {"cls": z}).wait_recv()
    for k in range(own):
        total = PRIOR_WEIGHT * own_ref[k].astype(F32) + share[me_z, k].astype(F32)
        for z in peers_z:
            total = total + deep[z, k].astype(F32)
        out_ref[k] = total / (PRIOR_WEIGHT + w_mine[k : k + 1, 0:1])
    for made in sends:
        made.wait_send()


def reduce_update(sums, weights, references):
    owners, lanes, chips, own, rows, tile_len = sums.shape
    slots = weights.shape[1:]
    piece = (own, rows, tile_len)
    dma = pltpu.SemaphoreType.DMA
    return pl.pallas_call(
        reduce_kernel,
        out_shape=jax.ShapeDtypeStruct(references.shape, F32),
        in_specs=[pl.BlockSpec(memory_space=pl.ANY)] + [pl.BlockSpec(memory_space=pltpu.VMEM)] * 2,
        out_specs=pl.BlockSpec(memory_space=pltpu.VMEM),
        scratch_shapes=[
            pltpu.VMEM((owners, chips) + piece, BF16),
            pltpu.VMEM((chips, owners) + piece, BF16),
            pltpu.VMEM((owners,) + piece, BF16),
            pltpu.VMEM((owners,) + piece, BF16),
            pltpu.VMEM((owners,) + slots, F32),
            pltpu.VMEM((chips, owners) + slots, F32),
            pltpu.VMEM((owners,) + slots, F32),
            pltpu.VMEM((owners,) + slots, F32),
            pltpu.VMEM((owners, chips) + piece, BF16),
            dma((owners,)),
            dma((2, owners)),
            dma((chips, owners)),
            dma((chips, owners)),
            dma((owners,)),
            dma((owners,)),
            dma((2,)),
            dma((chips,)),
            dma((chips,)),
            dma((owners,)),
            dma((owners,)),
        ],
        compiler_params=pltpu.CompilerParams(
            collective_id=1, has_side_effects=True, vmem_limit_bytes=56 * MIB
        ),
        name="reduce_update",
    )(sums, weights, references)


def local(particles, classes, rotation, defocus, filter_taps, ctf_table, references):
    owners = lax.axis_size("cls")
    reps = lax.axis_size("rep")
    own, rows, tile_len = references.shape
    stack = (owners, 2, reps // 2)
    small = reps % 2 == 0 and owners * reps * references.size <= 4 * MIB
    tiles = (particles, rotation, defocus, filter_taps, ctf_table, references)
    if small:
        filtered, refs = filter_tiles(*tiles, stack)
        sums, weights = weigh(filtered, classes, refs)
        return reduce_update(sums, weights, references)
    refs = lax.all_gather(references, ("cls", "rep"), axis=0, tiled=False)
    [filtered] = filter_tiles(*tiles, None)
    refs = refs.reshape(owners, 1, reps, own, rows, tile_len)
    sums, weights = weigh(filtered, classes, refs)
    sums = sums[:, 0]
    sums = lax.psum_scatter(sums, "rep", scatter_dimension=1, tiled=False)
    sums = lax.psum_scatter(sums, "cls", scatter_dimension=0, tiled=False)
    weights = lax.psum(weights[:, :own, 0], ("cls", "rep"))
    total = lax.dynamic_index_in_dim(weights, lax.axis_index("cls"), 0, keepdims=False)
    return (PRIOR_WEIGHT * references.astype(F32) + sums.astype(F32)) / (
        PRIOR_WEIGHT + total[:, None, None]
    )


def solution(mesh):
    placed = (
        P(("groups", "cls", "rep"), None, None),
        P(("groups", "cls", "rep")),
        P(("groups", "cls", "rep")),
        P(("groups", "cls", "rep")),
        P(),
        P(),
        P(("groups", "cls"), "rep", None),
    )
    return jax.shard_map(
        local,
        mesh=mesh,
        in_specs=placed,
        out_specs=P(("groups", "cls"), "rep", None),
        check_vma=False,
    )
```

```python
import functools
import math

import numpy as np

import jax
import jax.numpy as jnp
from jax import lax
from jax.experimental import pallas as pl
from jax.experimental.pallas import tpu as pltpu
from jax.sharding import PartitionSpec as P

EPSILON = 1e-05
PRIOR_WEIGHT = 4.0
F32 = jnp.float32
BF16 = jnp.bfloat16
MIB = 1 << 20


def hartley_table(tile_len):
    index = np.arange(tile_len, dtype=np.int64)
    phases = 2.0 * np.pi / tile_len * (index[:, None] * index[None, :] % tile_len)
    return (np.cos(phases) + np.sin(phases)).astype(np.float32)


def remote(src, dst, send, recv, device):
    return pltpu.make_async_remote_copy(
        src_ref=src,
        dst_ref=dst,
        send_sem=send,
        recv_sem=recv,
        device_id=device,
        device_id_type=pl.DeviceIdType.MESH,
    )


def enter(devices):
    barrier = pltpu.get_barrier_semaphore()
    for device in devices:
        pl.semaphore_signal(
            barrier, inc=1, device_id=device, device_id_type=pl.DeviceIdType.MESH
        )
    pl.semaphore_wait(barrier, len(devices))


def gather_steps(own_ref, all_ref, sems):
    keep, z_send, z_recv, x_send, x_recv, t_send, t_recv = sems
    owners, lanes, chips = all_ref.shape[:3]
    me_z = lax.axis_index("cls")
    rep = lax.axis_index("rep")
    me_x, lane = rep // lanes, rep % lanes
    twin = {"rep": me_x * lanes + (1 - lane)}
    next_x = [(me_x + d) % chips for d in range(1, chips)]
    held = all_ref.at[me_z, lane, me_x]
    has_left, has_right = me_z > 0, me_z < owners - 1

    def to_x(x):
        return {"rep": x * lanes + lane}

    def along_z(src, z, way):
        return remote(
            src,
            all_ref.at[z, lane, me_x],
            z_send.at[way, z],
            z_recv.at[z],
            {"cls": me_z + 1 if way else me_z - 1},
        )

    def across_x(src, x, z, slot):
        return remote(src, all_ref.at[z, lane, slot], x_send.at[x, z], x_recv.at[slot, z], to_x(x))

    def across_twin(src, z, x):
        return remote(src, all_ref.at[z, lane, x], t_send.at[x, z], t_recv.at[x, z], twin)

    def begin():
        others = [{"cls": (me_z + d) % owners} for d in range(1, owners)]
        enter([twin] + [to_x(x) for x in next_x] + others)
        pl.when(has_right)(lambda: along_z(own_ref, me_z, 1).start())
        pl.when(has_left)(lambda: along_z(own_ref, me_z, 0).start())
        for x in next_x:
            across_x(own_ref, x, me_z, me_x).start()
        across_twin(own_ref, me_z, me_x).start()
        pltpu.make_async_copy(own_ref, held, keep).start()

    def sides(distance):
        low, high = me_z - distance, me_z + distance
        return [(low >= 0, low, has_right, 1), (high < owners, high, has_left, 0)]

    def pass_z(distance):
        for there, z, onward, way in sides(distance):

            @pl.when(there)
            def _(z=z, onward=onward, way=way):
                src = all_ref.at[z, lane, me_x]
                along_z(own_ref, z, way).wait_recv()
                pl.when(onward)(lambda: along_z(src, z, way).start())
                for x in next_x:
                    across_x(src, x, z, me_x).start()
                across_twin(src, z, me_x).start()

    def pass_x(z):
        for x in next_x:
            across_x(own_ref, x, z, x).wait_recv()
            across_twin(all_ref.at[z, lane, x], z, x).start()

    def pass_x_side(distance, side):
        there, z, _, _ = sides(distance)[side]
        pl.when(there)(lambda: pass_x(z))

    def finish():
        pltpu.make_async_copy(own_ref, held, keep).wait()
        for z in range(owners):
            for x in [me_x] + next_x:
                remote(
                    own_ref, all_ref.at[z, 1 - lane, x], t_send.at[x, z], t_recv.at[x, z], twin
                ).wait()
            for x in next_x:
                across_x(own_ref, x, z, me_x).wait_send()
        pl.when(has_right)(lambda: along_z(own_ref, me_z, 1).wait_send())
        pl.when(has_left)(lambda: along_z(own_ref, me_z, 0).wait_send())
        for distance in range(1, owners):
            for there, z, onward, way in sides(distance):
                pl.when(there & onward)(
                    functools.partial(lambda z, way: along_z(own_ref, z, way).wait_send(), z, way)
                )

    stages = [(0, begin), (5, functools.partial(pass_x, me_z))]
    for d in range(1, owners):
        stages.append((4 * d, functools.partial(pass_z, d)))
        stages.append((4 * d + 5, functools.partial(pass_x_side, d, 0)))
        stages.append((4 * d + 7, functools.partial(pass_x_side, d, 1)))
    stages.sort(key=lambda entry: entry[0])
    return stages + [(1 << 20, finish)]


def filter_kernel(
    turn_ref, bin_ref, taps_ref, hartley_ref, ctf_ref, tile_ref, *rest
):
    if len(rest) > 4:
        own_ref, out_ref, all_ref, fwd, fwd_t, syn = rest[:6]
        stages = gather_steps(own_ref, all_ref, rest[6:])
    else:
        out_ref, fwd, fwd_t, syn = rest
        stages = []
    batch, tile_len, _ = tile_ref.shape
    taps = taps_ref.shape[0]
    half = (taps - 1) // 2
    step = pl.program_id(0)
    steps = pl.num_programs(0)

    @pl.when(step == 0)
    def _():
        if stages:
            stages[0][1]()
        row = lax.broadcasted_iota(jnp.int32, (tile_len, tile_len), 0)
        col = lax.broadcasted_iota(jnp.int32, (tile_len, tile_len), 1)
        gap = col - row
        band = jnp.zeros((tile_len, tile_len), F32)
        for tap in range(taps):
            band = jnp.where(gap == tap - half, taps_ref[tap], band)
        hartley = hartley_ref[...]
        analysis = jnp.dot(
            hartley, band, preferred_element_type=F32, precision=lax.Precision.HIGHEST
        ).astype(BF16)
        mirror = jnp.where(row + col == tile_len - 1, 1.0, 0.0).astype(BF16)
        mirrored = jnp.dot(analysis, mirror, preferred_element_type=F32)
        fwd[0] = analysis
        fwd[1] = mirrored.astype(BF16)
        fwd_t[0] = analysis.astype(F32).T.astype(BF16)
        fwd_t[1] = mirrored.T.astype(BF16)
        syn[...] = hartley.astype(BF16)

    for i in range(batch):
        code = turn_ref[step * batch + i]
        tile = tile_ref[i]
        tile = jnp.where(code >= 4, tile.T, tile)
        first = jnp.dot(tile, fwd_t[(code // 2) % 2], preferred_element_type=F32).astype(BF16)
        raw = jnp.dot(fwd[code % 2], first, preferred_element_type=F32)
        gain = ctf_ref[bin_ref[step * batch + i]].astype(F32)
        spectra = (raw * gain).astype(BF16)
        second = jnp.dot(spectra, syn[...], preferred_element_type=F32).astype(BF16)
        result = jnp.dot(syn[...], second, preferred_element_type=F32)
        out_ref[i] = (result * (1.0 / (tile_len * tile_len))).astype(BF16)

    for at, stage in stages[1:]:

        @pl.when(step == jnp.minimum(at, steps - 1))
        def _(stage=stage):
            stage()


def filter_tiles(particles, rotation, defocus, filter_taps, ctf_table, references, gather):
    count, tile_len, _ = particles.shape
    batch = math.gcd(count, 2)
    hartley = jnp.asarray(hartley_table(tile_len))
    square = (tile_len, tile_len)
    in_specs = [pl.BlockSpec(memory_space=pltpu.SMEM)] * 3 + [
        pl.BlockSpec(square, lambda i: (0, 0)),
        pl.BlockSpec(ctf_table.shape, lambda i: (0, 0, 0)),
        pl.BlockSpec((batch,) + square, lambda i: (i, 0, 0)),
    ]
    out_specs = [pl.BlockSpec((batch,) + square, lambda i: (i, 0, 0))]
    out_shape = [jax.ShapeDtypeStruct(particles.shape, BF16)]
    scratch = [
        pltpu.VMEM((2,) + square, BF16),
        pltpu.VMEM((2,) + square, BF16),
        pltpu.VMEM(square, BF16),
    ]
    operands = [rotation, defocus, filter_taps, hartley, ctf_table, particles]
    params = dict(vmem_limit_bytes=56 * MIB)
    if gather:
        owners, lanes, chips = gather
        dma = pltpu.SemaphoreType.DMA
        in_specs.append(pl.BlockSpec(memory_space=pl.ANY))
        out_specs.append(pl.BlockSpec(memory_space=pl.ANY))
        out_shape.append(jax.ShapeDtypeStruct(gather + references.shape, BF16))
        scratch += [
            dma,
            dma((2, owners)),
            dma((owners,)),
            dma((chips, owners)),
            dma((chips, owners)),
            dma((chips, owners)),
            dma((chips, owners)),
        ]
        operands.append(references)
        params.update(collective_id=2, has_side_effects=True)
    return pl.pallas_call(
        filter_kernel,
        grid=(count // batch,),
        in_specs=in_specs,
        out_specs=out_specs,
        scratch_shapes=scratch,
        out_shape=out_shape,
        compiler_params=pltpu.CompilerParams(**params),
        cost_estimate=pl.CostEstimate(
            flops=8 * count * tile_len**3,
            bytes_accessed=4 * count * tile_len**2,
            transcendentals=0,
        ),
        name="filter_tiles",
    )(*operands)


def weigh_kernel(
    class_ref, tile_ref, refs_ref, sum_ref, weight_ref, acc, parts, weigh_by, scale_by,
    start, order
):
    count, tile_len, _ = tile_ref.shape
    _, lanes, chips, own, rows, _ = refs_ref.shape
    reps = lanes * chips
    owners = pl.num_programs(0)
    owner = pl.program_id(0)
    scale = 1.0 / (tile_len * tile_len)

    @pl.when(owner == 0)
    def _():
        def clear(i, carry):
            start[i] = 0
            return carry

        lax.fori_loop(0, owners + 1, clear, 0)

        def tally(i, carry):
            slot = class_ref[i] // own + 1
            start[slot] = start[slot] + 1
            return carry

        lax.fori_loop(0, count, tally, 0)

        def running(i, carry):
            total = carry + start[i]
            start[i] = total
            return total

        lax.fori_loop(0, owners + 1, running, 0)

        def place(i, carry):
            slot = class_ref[i] // own
            where = start[slot]
            order[where] = i
            start[slot] = where + 1
            return carry

        lax.fori_loop(0, count, place, 0)

    end = start[owner]
    begin = jnp.where(owner == 0, 0, start[jnp.maximum(owner - 1, 0)])
    acc[...] = jnp.zeros_like(acc)
    weight_ref[...] = jnp.zeros_like(weight_ref)
    row = lax.broadcasted_iota(jnp.int32, weight_ref.shape[1:], 0)

    def fold(values):
        tall = jnp.sum(values.reshape(rows // 8, 8, tile_len), axis=0)
        return sum(tall[:, at : at + 128] for at in range(0, tile_len, 128))

    def gather_parts(i, carry):
        p = order[i]
        k = class_ref[p] - owner * own
        power = ref_power = meet = jnp.zeros((8, 128), F32)
        for rep in range(reps):
            tile = tile_ref[p, rep * rows : (rep + 1) * rows].astype(F32)
            image = refs_ref[0, rep % lanes, rep // lanes, k].astype(F32)
            power = power + fold(tile * tile)
            ref_power = ref_power + fold(image * image)
            meet = meet + fold(tile * image)
        parts[0, i] = power
        parts[1, i] = ref_power
        parts[2, i] = meet
        return carry

    lax.fori_loop(begin, end, gather_parts, 0)

    def total(which):
        return jnp.sum(jnp.sum(parts[which], axis=1), axis=1, keepdims=True) * scale

    power, ref_power, meet = total(0), total(1), total(2)
    score = meet / jnp.sqrt((power + EPSILON) * (ref_power + EPSILON))
    weight = 1.0 / (1.0 + jnp.exp(-tile_len * score))
    scaling = (weight / jnp.sqrt(power + EPSILON)).astype(BF16).astype(F32)
    weigh_by[...] = jnp.broadcast_to(weight, weigh_by.shape)
    scale_by[...] = jnp.broadcast_to(scaling, scale_by.shape)

    def add_tile(i, carry):
        p = order[i]
        k = class_ref[p] - owner * own
        factor = jnp.broadcast_to(scale_by[pl.ds(i, 1), :], (rows, 128))
        factor = jnp.concatenate([factor] * (tile_len // 128), axis=1)
        for rep in range(reps):
            part = pl.ds(rep * rows, rows)
            acc[k, part] += factor * tile_ref[p, part].astype(F32)
        weight_ref[0] += jnp.where(row == k, weigh_by[pl.ds(i, 1), :], 0.0)
        return carry

    lax.fori_loop(begin, end, add_tile, 0)
    for k in range(own):
        whole = acc[k].astype(BF16).reshape(reps, rows, tile_len)
        for rep in range(reps):
            sum_ref[0, rep % lanes, rep // lanes, k] = whole[rep]


def weigh(filtered, classes, refs):
    count, tile_len, _ = filtered.shape
    owners, lanes, chips, own, rows, _ = refs.shape
    slots = -(-own // 8) * 8
    block = (1,) + refs.shape[1:]
    grid_spec = pltpu.PrefetchScalarGridSpec(
        num_scalar_prefetch=1,
        grid=(owners,),
        in_specs=[
            pl.BlockSpec(filtered.shape, lambda o, *_: (0, 0, 0)),
            pl.BlockSpec(block, lambda o, *_: (o, 0, 0, 0, 0, 0)),
        ],
        out_specs=[
            pl.BlockSpec(block, lambda o, *_: (o, 0, 0, 0, 0, 0)),
            pl.BlockSpec((1, slots, 128), lambda o, *_: (o, 0, 0)),
        ],
        scratch_shapes=[
            pltpu.VMEM((own, tile_len, tile_len), F32),
            pltpu.VMEM((3, count, 8, 128), F32),
            pltpu.VMEM((count, 128), F32),
            pltpu.VMEM((count, 128), F32),
            pltpu.SMEM((owners + 1,), jnp.int32),
            pltpu.SMEM((count,), jnp.int32),
        ],
    )
    return pl.pallas_call(
        weigh_kernel,
        grid_spec=grid_spec,
        out_shape=[
            jax.ShapeDtypeStruct(refs.shape, BF16),
            jax.ShapeDtypeStruct((owners, slots, 128), F32),
        ],
        compiler_params=pltpu.CompilerParams(vmem_limit_bytes=56 * MIB),
        name="weigh_tiles",
    )(classes, filtered, refs)


def reduce_kernel(
    sum_ref, weight_ref, own_ref, out_ref, near, far, share, deep, w_near, w_far, w_share, w_deep,
    kept, keep, near_sem, far_send, far_recv, deep_send, deep_recv, wn_sem, wf_send, wf_recv, wd_send, wd_recv
):
    owners, lanes, chips, own, rows, _ = sum_ref.shape
    me_z = lax.axis_index("cls")
    rep = lax.axis_index("rep")
    me_x, lane = rep // lanes, rep % lanes
    twin = {"rep": me_x * lanes + (1 - lane)}
    peers_x = [(me_x + d) % chips for d in range(1, chips)]
    peers_z = [(me_z + d) % owners for d in range(1, owners)]

    def copy(src, dst, send, recv, device):
        return pltpu.make_async_remote_copy(
            src_ref=src,
            dst_ref=dst,
            send_sem=send,
            recv_sem=recv,
            device_id=device,
            device_id_type=pl.DeviceIdType.MESH,
        )

    def to_x(x):
        return {"rep": x * lanes + lane}

    barrier = pltpu.get_barrier_semaphore()
    for device in [twin] + [to_x(x) for x in peers_x] + [{"cls": z} for z in peers_z]:
        pl.semaphore_signal(
            barrier, inc=1, device_id=device, device_id_type=pl.DeviceIdType.MESH
        )
    pl.semaphore_wait(barrier, chips + owners - 1)

    sends = []

    def launch(made):
        made.start()
        sends.append(made)

    order = peers_z + [me_z]
    launch(copy(weight_ref, w_near, wn_sem.at[0], wn_sem.at[1], twin))
    for o in order:
        launch(copy(sum_ref.at[o, 1 - lane], near.at[o], near_sem.at[0, o], near_sem.at[1, o], twin))

    for o in order:
        pltpu.make_async_copy(sum_ref.at[o, lane], kept.at[o], keep.at[o]).start()
    copy(weight_ref, w_near, wn_sem.at[0], wn_sem.at[1], twin).wait_recv()
    w_share[...] = weight_ref[...] + w_near[...]
    for x in peers_x:
        launch(copy(w_share, w_far.at[me_x], wf_send.at[x], wf_recv.at[me_x], to_x(x)))
    for o in order:
        copy(
            sum_ref.at[o, lane], near.at[o], near_sem.at[0, o], near_sem.at[1, o], twin
        ).wait_recv()
        pltpu.make_async_copy(sum_ref.at[o, lane], kept.at[o], keep.at[o]).wait()
        near[o] = (near[o].astype(F32) + kept[o].astype(F32)).astype(BF16)
        for x in peers_x:
            launch(
                copy(near.at[o, x], far.at[me_x, o], far_send.at[x, o], far_recv.at[me_x, o], to_x(x))
            )
    w_total = w_share[...]
    for x in peers_x:
        copy(w_share, w_far.at[x], wf_send.at[x], wf_recv.at[x], to_x(x)).wait_recv()
        w_total = w_total + w_far[x]
    for x in peers_x:
        made = copy(w_share, w_far.at[me_x], wf_send.at[x], wf_recv.at[me_x], to_x(x))
        made.wait_send()
        sends.pop(1 + owners)
    w_share[...] = w_total
    for z in peers_z:
        launch(copy(w_share.at[z], w_deep.at[me_z], wd_send.at[z], wd_recv.at[me_z], {"cls": z}))
    for o in order:
        total = near[o, me_x].astype(F32)
        for x in peers_x:
            copy(near.at[o, x], far.at[x, o], far_send.at[x, o], far_recv.at[x, o], to_x(x)).wait_recv()
            total = total + far[x, o].astype(F32)
        share[o] = total.astype(BF16)
        if o is not me_z:
            launch(copy(share.at[o], deep.at[me_z], deep_send.at[o], deep_recv.at[me_z], {"cls": o}))
    w_mine = w_share[me_z]
    for z in peers_z:
        copy(w_share.at[z], w_deep.at[z], wd_send.at[z], wd_recv.at[z], {"cls": z}).wait_recv()
        w_mine = w_mine + w_deep[z]
    for z in peers_z:
        copy(share.at[z], deep.at[z], deep_send.at[z], deep_recv.at[z], {"cls": z}).wait_recv()
    for k in range(own):
        total = PRIOR_WEIGHT * own_ref[k].astype(F32) + share[me_z, k].astype(F32)
        for z in peers_z:
            total = total + deep[z, k].astype(F32)
        out_ref[k] = total / (PRIOR_WEIGHT + w_mine[k : k + 1, 0:1])
    for made in sends:
        made.wait_send()


def reduce_update(sums, weights, references):
    owners, lanes, chips, own, rows, tile_len = sums.shape
    slots = weights.shape[1:]
    piece = (own, rows, tile_len)
    dma = pltpu.SemaphoreType.DMA
    return pl.pallas_call(
        reduce_kernel,
        out_shape=jax.ShapeDtypeStruct(references.shape, F32),
        in_specs=[pl.BlockSpec(memory_space=pl.ANY)] + [pl.BlockSpec(memory_space=pltpu.VMEM)] * 2,
        out_specs=pl.BlockSpec(memory_space=pltpu.VMEM),
        scratch_shapes=[
            pltpu.VMEM((owners, chips) + piece, BF16),
            pltpu.VMEM((chips, owners) + piece, BF16),
            pltpu.VMEM((owners,) + piece, BF16),
            pltpu.VMEM((owners,) + piece, BF16),
            pltpu.VMEM((owners,) + slots, F32),
            pltpu.VMEM((chips, owners) + slots, F32),
            pltpu.VMEM((owners,) + slots, F32),
            pltpu.VMEM((owners,) + slots, F32),
            pltpu.VMEM((owners, chips) + piece, BF16),
            dma((owners,)),
            dma((2, owners)),
            dma((chips, owners)),
            dma((chips, owners)),
            dma((owners,)),
            dma((owners,)),
            dma((2,)),
            dma((chips,)),
            dma((chips,)),
            dma((owners,)),
            dma((owners,)),
        ],
        compiler_params=pltpu.CompilerParams(
            collective_id=1, has_side_effects=True, vmem_limit_bytes=32 * MIB
        ),
        name="reduce_update",
    )(sums, weights, references)


def local(particles, classes, rotation, defocus, filter_taps, ctf_table, references):
    owners = lax.axis_size("cls")
    reps = lax.axis_size("rep")
    own, rows, tile_len = references.shape
    stack = (owners, 2, reps // 2)
    small = reps % 2 == 0 and owners * reps * references.size <= 4 * MIB
    tiles = (particles, rotation, defocus, filter_taps, ctf_table, references)
    if small:
        filtered, refs = filter_tiles(*tiles, stack)
        sums, weights = weigh(filtered, classes, refs)
        return reduce_update(sums, weights, references)
    refs = lax.all_gather(references, ("cls", "rep"), axis=0, tiled=False)
    [filtered] = filter_tiles(*tiles, None)
    refs = refs.reshape(owners, 1, reps, own, rows, tile_len)
    sums, weights = weigh(filtered, classes, refs)
    sums = sums[:, 0]
    sums = lax.psum_scatter(sums, "rep", scatter_dimension=1, tiled=False)
    sums = lax.psum_scatter(sums, "cls", scatter_dimension=0, tiled=False)
    weights = lax.psum(weights[:, :own, 0], ("cls", "rep"))
    total = lax.dynamic_index_in_dim(weights, lax.axis_index("cls"), 0, keepdims=False)
    return (PRIOR_WEIGHT * references.astype(F32) + sums.astype(F32)) / (
        PRIOR_WEIGHT + total[:, None, None]
    )


def solution(mesh):
    placed = (
        P(("groups", "cls", "rep"), None, None),
        P(("groups", "cls", "rep")),
        P(("groups", "cls", "rep")),
        P(("groups", "cls", "rep")),
        P(),
        P(),
        P(("groups", "cls"), "rep", None),
    )
    return jax.shard_map(
        local,
        mesh=mesh,
        in_specs=placed,
        out_specs=P(("groups", "cls"), "rep", None),
        check_vma=False,
    )
```

```python
import functools
import math

import numpy as np

import jax
import jax.numpy as jnp
from jax import lax
from jax.experimental import pallas as pl
from jax.experimental.pallas import tpu as pltpu
from jax.sharding import PartitionSpec as P

EPSILON = 1e-05
PRIOR_WEIGHT = 4.0
F32 = jnp.float32
BF16 = jnp.bfloat16
MIB = 1 << 20


def hartley_table(tile_len):
    index = np.arange(tile_len, dtype=np.int64)
    phases = 2.0 * np.pi / tile_len * (index[:, None] * index[None, :] % tile_len)
    return (np.cos(phases) + np.sin(phases)).astype(np.float32)


def remote(src, dst, send, recv, device):
    return pltpu.make_async_remote_copy(
        src_ref=src,
        dst_ref=dst,
        send_sem=send,
        recv_sem=recv,
        device_id=device,
        device_id_type=pl.DeviceIdType.MESH,
    )


def enter(devices):
    barrier = pltpu.get_barrier_semaphore()
    for device in devices:
        pl.semaphore_signal(
            barrier, inc=1, device_id=device, device_id_type=pl.DeviceIdType.MESH
        )
    pl.semaphore_wait(barrier, len(devices))


def gather_steps(own_ref, all_ref, sems):
    keep, z_send, z_recv, x_send, x_recv, t_send, t_recv = sems
    owners, lanes, chips = all_ref.shape[:3]
    me_z = lax.axis_index("cls")
    rep = lax.axis_index("rep")
    me_x, lane = rep // lanes, rep % lanes
    twin = {"rep": me_x * lanes + (1 - lane)}
    next_x = [(me_x + d) % chips for d in range(1, chips)]
    held = all_ref.at[me_z, lane, me_x]
    has_left, has_right = me_z > 0, me_z < owners - 1

    def to_x(x):
        return {"rep": x * lanes + lane}

    def along_z(src, z, way):
        return remote(
            src,
            all_ref.at[z, lane, me_x],
            z_send.at[way, z],
            z_recv.at[z],
            {"cls": me_z + 1 if way else me_z - 1},
        )

    def across_x(src, x, z, slot):
        return remote(src, all_ref.at[z, lane, slot], x_send.at[x, z], x_recv.at[slot, z], to_x(x))

    def across_twin(src, z, x):
        return remote(src, all_ref.at[z, lane, x], t_send.at[x, z], t_recv.at[x, z], twin)

    def begin():
        others = [{"cls": (me_z + d) % owners} for d in range(1, owners)]
        enter([twin] + [to_x(x) for x in next_x] + others)
        pl.when(has_right)(lambda: along_z(own_ref, me_z, 1).start())
        pl.when(has_left)(lambda: along_z(own_ref, me_z, 0).start())
        for x in next_x:
            across_x(own_ref, x, me_z, me_x).start()
        across_twin(own_ref, me_z, me_x).start()
        pltpu.make_async_copy(own_ref, held, keep).start()

    def sides(distance):
        low, high = me_z - distance, me_z + distance
        return [(low >= 0, low, has_right, 1), (high < owners, high, has_left, 0)]

    def pass_z(distance):
        for there, z, onward, way in sides(distance):

            @pl.when(there)
            def _(z=z, onward=onward, way=way):
                src = all_ref.at[z, lane, me_x]
                along_z(own_ref, z, way).wait_recv()
                pl.when(onward)(lambda: along_z(src, z, way).start())
                for x in next_x:
                    across_x(src, x, z, me_x).start()
                across_twin(src, z, me_x).start()

    def pass_x(z):
        for x in next_x:
            across_x(own_ref, x, z, x).wait_recv()
            across_twin(all_ref.at[z, lane, x], z, x).start()

    def pass_x_side(distance, side):
        there, z, _, _ = sides(distance)[side]
        pl.when(there)(lambda: pass_x(z))

    def finish():
        pltpu.make_async_copy(own_ref, held, keep).wait()
        for z in range(owners):
            for x in [me_x] + next_x:
                remote(
                    own_ref, all_ref.at[z, 1 - lane, x], t_send.at[x, z], t_recv.at[x, z], twin
                ).wait()
            for x in next_x:
                across_x(own_ref, x, z, me_x).wait_send()
        pl.when(has_right)(lambda: along_z(own_ref, me_z, 1).wait_send())
        pl.when(has_left)(lambda: along_z(own_ref, me_z, 0).wait_send())
        for distance in range(1, owners):
            for there, z, onward, way in sides(distance):
                pl.when(there & onward)(
                    functools.partial(lambda z, way: along_z(own_ref, z, way).wait_send(), z, way)
                )

    stages = [(0, begin), (5, functools.partial(pass_x, me_z))]
    for d in range(1, owners):
        stages.append((4 * d, functools.partial(pass_z, d)))
        stages.append((4 * d + 5, functools.partial(pass_x_side, d, 0)))
        stages.append((4 * d + 7, functools.partial(pass_x_side, d, 1)))
    stages.sort(key=lambda entry: entry[0])
    return stages + [(1 << 20, finish)]


def filter_kernel(
    turn_ref, bin_ref, taps_ref, hartley_ref, ctf_ref, tile_ref, *rest
):
    if len(rest) > 4:
        own_ref, out_ref, all_ref, fwd, fwd_t, syn = rest[:6]
        stages = gather_steps(own_ref, all_ref, rest[6:])
    else:
        out_ref, fwd, fwd_t, syn = rest
        stages = []
    batch, tile_len, _ = tile_ref.shape
    taps = taps_ref.shape[0]
    half = (taps - 1) // 2
    step = pl.program_id(0)
    steps = pl.num_programs(0)

    @pl.when(step == 0)
    def _():
        if stages:
            stages[0][1]()
        row = lax.broadcasted_iota(jnp.int32, (tile_len, tile_len), 0)
        col = lax.broadcasted_iota(jnp.int32, (tile_len, tile_len), 1)
        gap = col - row
        band = jnp.zeros((tile_len, tile_len), F32)
        for tap in range(taps):
            band = jnp.where(gap == tap - half, taps_ref[tap], band)
        hartley = hartley_ref[...]
        analysis = jnp.dot(
            hartley, band, preferred_element_type=F32, precision=lax.Precision.HIGHEST
        ).astype(BF16)
        mirror = jnp.where(row + col == tile_len - 1, 1.0, 0.0).astype(BF16)
        mirrored = jnp.dot(analysis, mirror, preferred_element_type=F32)
        fwd[0] = analysis
        fwd[1] = mirrored.astype(BF16)
        fwd_t[0] = analysis.astype(F32).T.astype(BF16)
        fwd_t[1] = mirrored.T.astype(BF16)
        syn[...] = hartley.astype(BF16)

    for i in range(batch):
        code = turn_ref[step * batch + i]
        tile = tile_ref[i]
        tile = jnp.where(code >= 4, tile.T, tile)
        first = jnp.dot(tile, fwd_t[(code // 2) % 2], preferred_element_type=F32).astype(BF16)
        raw = jnp.dot(fwd[code % 2], first, preferred_element_type=F32)
        gain = ctf_ref[bin_ref[step * batch + i]].astype(F32)
        spectra = (raw * gain).astype(BF16)
        second = jnp.dot(spectra, syn[...], preferred_element_type=F32).astype(BF16)
        result = jnp.dot(syn[...], second, preferred_element_type=F32)
        out_ref[i] = (result * (1.0 / (tile_len * tile_len))).astype(BF16)

    for at, stage in stages[1:]:

        @pl.when(step == jnp.minimum((at + 1) // 2, steps - 1))
        def _(stage=stage):
            stage()


def filter_tiles(particles, rotation, defocus, filter_taps, ctf_table, references, gather):
    count, tile_len, _ = particles.shape
    batch = math.gcd(count, 4)
    hartley = jnp.asarray(hartley_table(tile_len))
    square = (tile_len, tile_len)
    in_specs = [pl.BlockSpec(memory_space=pltpu.SMEM)] * 3 + [
        pl.BlockSpec(square, lambda i: (0, 0)),
        pl.BlockSpec(ctf_table.shape, lambda i: (0, 0, 0)),
        pl.BlockSpec((batch,) + square, lambda i: (i, 0, 0)),
    ]
    out_specs = [pl.BlockSpec((batch,) + square, lambda i: (i, 0, 0))]
    out_shape = [jax.ShapeDtypeStruct(particles.shape, BF16)]
    scratch = [
        pltpu.VMEM((2,) + square, BF16),
        pltpu.VMEM((2,) + square, BF16),
        pltpu.VMEM(square, BF16),
    ]
    operands = [rotation, defocus, filter_taps, hartley, ctf_table, particles]
    params = dict(vmem_limit_bytes=56 * MIB)
    if gather:
        owners, lanes, chips = gather
        dma = pltpu.SemaphoreType.DMA
        in_specs.append(pl.BlockSpec(memory_space=pl.ANY))
        out_specs.append(pl.BlockSpec(memory_space=pl.ANY))
        out_shape.append(jax.ShapeDtypeStruct(gather + references.shape, BF16))
        scratch += [
            dma,
            dma((2, owners)),
            dma((owners,)),
            dma((chips, owners)),
            dma((chips, owners)),
            dma((chips, owners)),
            dma((chips, owners)),
        ]
        operands.append(references)
        params.update(collective_id=2, has_side_effects=True)
    return pl.pallas_call(
        filter_kernel,
        grid=(count // batch,),
        in_specs=in_specs,
        out_specs=out_specs,
        scratch_shapes=scratch,
        out_shape=out_shape,
        compiler_params=pltpu.CompilerParams(**params),
        cost_estimate=pl.CostEstimate(
            flops=8 * count * tile_len**3,
            bytes_accessed=4 * count * tile_len**2,
            transcendentals=0,
        ),
        name="filter_tiles",
    )(*operands)


def weigh_kernel(
    class_ref, tile_ref, refs_ref, sum_ref, weight_ref, acc, parts, weigh_by, scale_by,
    start, order
):
    count, tile_len, _ = tile_ref.shape
    _, lanes, chips, own, rows, _ = refs_ref.shape
    reps = lanes * chips
    owners = pl.num_programs(0)
    owner = pl.program_id(0)
    scale = 1.0 / (tile_len * tile_len)

    @pl.when(owner == 0)
    def _():
        def clear(i, carry):
            start[i] = 0
            return carry

        lax.fori_loop(0, owners + 1, clear, 0)

        def tally(i, carry):
            slot = class_ref[i] // own + 1
            start[slot] = start[slot] + 1
            return carry

        lax.fori_loop(0, count, tally, 0)

        def running(i, carry):
            total = carry + start[i]
            start[i] = total
            return total

        lax.fori_loop(0, owners + 1, running, 0)

        def place(i, carry):
            slot = class_ref[i] // own
            where = start[slot]
            order[where] = i
            start[slot] = where + 1
            return carry

        lax.fori_loop(0, count, place, 0)

    end = start[owner]
    begin = jnp.where(owner == 0, 0, start[jnp.maximum(owner - 1, 0)])
    acc[...] = jnp.zeros_like(acc)
    weight_ref[...] = jnp.zeros_like(weight_ref)
    row = lax.broadcasted_iota(jnp.int32, weight_ref.shape[1:], 0)

    def fold(values):
        tall = jnp.sum(values.reshape(rows // 8, 8, tile_len), axis=0)
        return sum(tall[:, at : at + 128] for at in range(0, tile_len, 128))

    def gather_parts(i, carry):
        p = order[i]
        k = class_ref[p] - owner * own
        power = ref_power = meet = jnp.zeros((8, 128), F32)
        for rep in range(reps):
            tile = tile_ref[p, rep * rows : (rep + 1) * rows].astype(F32)
            image = refs_ref[0, rep % lanes, rep // lanes, k].astype(F32)
            power = power + fold(tile * tile)
            ref_power = ref_power + fold(image * image)
            meet = meet + fold(tile * image)
        parts[0, i] = power
        parts[1, i] = ref_power
        parts[2, i] = meet
        return carry

    lax.fori_loop(begin, end, gather_parts, 0)

    def total(which):
        return jnp.sum(jnp.sum(parts[which], axis=1), axis=1, keepdims=True) * scale

    power, ref_power, meet = total(0), total(1), total(2)
    score = meet / jnp.sqrt((power + EPSILON) * (ref_power + EPSILON))
    weight = 1.0 / (1.0 + jnp.exp(-tile_len * score))
    scaling = (weight / jnp.sqrt(power + EPSILON)).astype(BF16).astype(F32)
    weigh_by[...] = jnp.broadcast_to(weight, weigh_by.shape)
    scale_by[...] = jnp.broadcast_to(scaling, scale_by.shape)

    def add_tile(i, carry):
        p = order[i]
        k = class_ref[p] - owner * own
        factor = jnp.broadcast_to(scale_by[pl.ds(i, 1), :], (rows, 128))
        factor = jnp.concatenate([factor] * (tile_len // 128), axis=1)
        for rep in range(reps):
            part = pl.ds(rep * rows, rows)
            acc[k, part] += factor * tile_ref[p, part].astype(F32)
        weight_ref[0] += jnp.where(row == k, weigh_by[pl.ds(i, 1), :], 0.0)
        return carry

    lax.fori_loop(begin, end, add_tile, 0)
    for k in range(own):
        whole = acc[k].astype(BF16).reshape(reps, rows, tile_len)
        for rep in range(reps):
            sum_ref[0, rep % lanes, rep // lanes, k] = whole[rep]


def weigh(filtered, classes, refs):
    count, tile_len, _ = filtered.shape
    owners, lanes, chips, own, rows, _ = refs.shape
    slots = -(-own // 8) * 8
    block = (1,) + refs.shape[1:]
    grid_spec = pltpu.PrefetchScalarGridSpec(
        num_scalar_prefetch=1,
        grid=(owners,),
        in_specs=[
            pl.BlockSpec(filtered.shape, lambda o, *_: (0, 0, 0)),
            pl.BlockSpec(block, lambda o, *_: (o, 0, 0, 0, 0, 0)),
        ],
        out_specs=[
            pl.BlockSpec(block, lambda o, *_: (o, 0, 0, 0, 0, 0)),
            pl.BlockSpec((1, slots, 128), lambda o, *_: (o, 0, 0)),
        ],
        scratch_shapes=[
            pltpu.VMEM((own, tile_len, tile_len), F32),
            pltpu.VMEM((3, count, 8, 128), F32),
            pltpu.VMEM((count, 128), F32),
            pltpu.VMEM((count, 128), F32),
            pltpu.SMEM((owners + 1,), jnp.int32),
            pltpu.SMEM((count,), jnp.int32),
        ],
    )
    return pl.pallas_call(
        weigh_kernel,
        grid_spec=grid_spec,
        out_shape=[
            jax.ShapeDtypeStruct(refs.shape, BF16),
            jax.ShapeDtypeStruct((owners, slots, 128), F32),
        ],
        compiler_params=pltpu.CompilerParams(vmem_limit_bytes=56 * MIB),
        name="weigh_tiles",
    )(classes, filtered, refs)


def reduce_kernel(
    sum_ref, weight_ref, own_ref, out_ref, near, far, share, deep, w_near, w_far, w_share, w_deep,
    kept, keep, near_sem, far_send, far_recv, deep_send, deep_recv, wn_sem, wf_send, wf_recv, wd_send, wd_recv
):
    owners, lanes, chips, own, rows, _ = sum_ref.shape
    me_z = lax.axis_index("cls")
    rep = lax.axis_index("rep")
    me_x, lane = rep // lanes, rep % lanes
    twin = {"rep": me_x * lanes + (1 - lane)}
    peers_x = [(me_x + d) % chips for d in range(1, chips)]
    peers_z = [(me_z + d) % owners for d in range(1, owners)]

    def copy(src, dst, send, recv, device):
        return pltpu.make_async_remote_copy(
            src_ref=src,
            dst_ref=dst,
            send_sem=send,
            recv_sem=recv,
            device_id=device,
            device_id_type=pl.DeviceIdType.MESH,
        )

    def to_x(x):
        return {"rep": x * lanes + lane}

    barrier = pltpu.get_barrier_semaphore()
    for device in [twin] + [to_x(x) for x in peers_x] + [{"cls": z} for z in peers_z]:
        pl.semaphore_signal(
            barrier, inc=1, device_id=device, device_id_type=pl.DeviceIdType.MESH
        )
    pl.semaphore_wait(barrier, chips + owners - 1)

    sends = []

    def launch(made):
        made.start()
        sends.append(made)

    order = peers_z + [me_z]
    launch(copy(weight_ref, w_near, wn_sem.at[0], wn_sem.at[1], twin))
    for o in order:
        launch(copy(sum_ref.at[o, 1 - lane], near.at[o], near_sem.at[0, o], near_sem.at[1, o], twin))

    for o in order:
        pltpu.make_async_copy(sum_ref.at[o, lane], kept.at[o], keep.at[o]).start()
    copy(weight_ref, w_near, wn_sem.at[0], wn_sem.at[1], twin).wait_recv()
    w_share[...] = weight_ref[...] + w_near[...]
    for x in peers_x:
        launch(copy(w_share, w_far.at[me_x], wf_send.at[x], wf_recv.at[me_x], to_x(x)))
    for o in order:
        copy(
            sum_ref.at[o, lane], near.at[o], near_sem.at[0, o], near_sem.at[1, o], twin
        ).wait_recv()
        pltpu.make_async_copy(sum_ref.at[o, lane], kept.at[o], keep.at[o]).wait()
        near[o] = (near[o].astype(F32) + kept[o].astype(F32)).astype(BF16)
        for x in peers_x:
            launch(
                copy(near.at[o, x], far.at[me_x, o], far_send.at[x, o], far_recv.at[me_x, o], to_x(x))
            )
    w_total = w_share[...]
    for x in peers_x:
        copy(w_share, w_far.at[x], wf_send.at[x], wf_recv.at[x], to_x(x)).wait_recv()
        w_total = w_total + w_far[x]
    for x in peers_x:
        made = copy(w_share, w_far.at[me_x], wf_send.at[x], wf_recv.at[me_x], to_x(x))
        made.wait_send()
        sends.pop(1 + owners)
    w_share[...] = w_total
    for z in peers_z:
        launch(copy(w_share.at[z], w_deep.at[me_z], wd_send.at[z], wd_recv.at[me_z], {"cls": z}))
    for o in order:
        total = near[o, me_x].astype(F32)
        for x in peers_x:
            copy(near.at[o, x], far.at[x, o], far_send.at[x, o], far_recv.at[x, o], to_x(x)).wait_recv()
            total = total + far[x, o].astype(F32)
        share[o] = total.astype(BF16)
        if o is not me_z:
            launch(copy(share.at[o], deep.at[me_z], deep_send.at[o], deep_recv.at[me_z], {"cls": o}))
    w_mine = w_share[me_z]
    for z in peers_z:
        copy(w_share.at[z], w_deep.at[z], wd_send.at[z], wd_recv.at[z], {"cls": z}).wait_recv()
        w_mine = w_mine + w_deep[z]
    for z in peers_z:
        copy(share.at[z], deep.at[z], deep_send.at[z], deep_recv.at[z], {"cls": z}).wait_recv()
    for k in range(own):
        total = PRIOR_WEIGHT * own_ref[k].astype(F32) + share[me_z, k].astype(F32)
        for z in peers_z:
            total = total + deep[z, k].astype(F32)
        out_ref[k] = total / (PRIOR_WEIGHT + w_mine[k : k + 1, 0:1])
    for made in sends:
        made.wait_send()


def reduce_update(sums, weights, references):
    owners, lanes, chips, own, rows, tile_len = sums.shape
    slots = weights.shape[1:]
    piece = (own, rows, tile_len)
    dma = pltpu.SemaphoreType.DMA
    return pl.pallas_call(
        reduce_kernel,
        out_shape=jax.ShapeDtypeStruct(references.shape, F32),
        in_specs=[pl.BlockSpec(memory_space=pl.ANY)] + [pl.BlockSpec(memory_space=pltpu.VMEM)] * 2,
        out_specs=pl.BlockSpec(memory_space=pltpu.VMEM),
        scratch_shapes=[
            pltpu.VMEM((owners, chips) + piece, BF16),
            pltpu.VMEM((chips, owners) + piece, BF16),
            pltpu.VMEM((owners,) + piece, BF16),
            pltpu.VMEM((owners,) + piece, BF16),
            pltpu.VMEM((owners,) + slots, F32),
            pltpu.VMEM((chips, owners) + slots, F32),
            pltpu.VMEM((owners,) + slots, F32),
            pltpu.VMEM((owners,) + slots, F32),
            pltpu.VMEM((owners, chips) + piece, BF16),
            dma((owners,)),
            dma((2, owners)),
            dma((chips, owners)),
            dma((chips, owners)),
            dma((owners,)),
            dma((owners,)),
            dma((2,)),
            dma((chips,)),
            dma((chips,)),
            dma((owners,)),
            dma((owners,)),
        ],
        compiler_params=pltpu.CompilerParams(
            collective_id=1, has_side_effects=True, vmem_limit_bytes=32 * MIB
        ),
        name="reduce_update",
    )(sums, weights, references)


def local(particles, classes, rotation, defocus, filter_taps, ctf_table, references):
    owners = lax.axis_size("cls")
    reps = lax.axis_size("rep")
    own, rows, tile_len = references.shape
    stack = (owners, 2, reps // 2)
    small = reps % 2 == 0 and owners * reps * references.size <= 4 * MIB
    tiles = (particles, rotation, defocus, filter_taps, ctf_table, references)
    if small:
        filtered, refs = filter_tiles(*tiles, stack)
        sums, weights = weigh(filtered, classes, refs)
        return reduce_update(sums, weights, references)
    refs = lax.all_gather(references, ("cls", "rep"), axis=0, tiled=False)
    [filtered] = filter_tiles(*tiles, None)
    refs = refs.reshape(owners, 1, reps, own, rows, tile_len)
    sums, weights = weigh(filtered, classes, refs)
    sums = sums[:, 0]
    sums = lax.psum_scatter(sums, "rep", scatter_dimension=1, tiled=False)
    sums = lax.psum_scatter(sums, "cls", scatter_dimension=0, tiled=False)
    weights = lax.psum(weights[:, :own, 0], ("cls", "rep"))
    total = lax.dynamic_index_in_dim(weights, lax.axis_index("cls"), 0, keepdims=False)
    return (PRIOR_WEIGHT * references.astype(F32) + sums.astype(F32)) / (
        PRIOR_WEIGHT + total[:, None, None]
    )


def solution(mesh):
    placed = (
        P(("groups", "cls", "rep"), None, None),
        P(("groups", "cls", "rep")),
        P(("groups", "cls", "rep")),
        P(("groups", "cls", "rep")),
        P(),
        P(),
        P(("groups", "cls"), "rep", None),
    )
    return jax.shard_map(
        local,
        mesh=mesh,
        in_specs=placed,
        out_specs=P(("groups", "cls"), "rep", None),
        check_vma=False,
    )
```
